128 devices in a mesh: rows: 16 (over y, z), cols: 8 (over x, core).
Axes of the slice: x: 4, y: 4, z: 4, core: 2. Of those that a mesh axis runs over, the one named last changes fastest.
Arguments:
- splat_map: float32 [12, 4194304], P(None, ('rows', 'cols')), may hold values from -8 to 8
- opacity: float32 [4194304], P(('rows', 'cols')), may hold values from 0.005 to 0.2
- depths: float32 [2, 4194304], P(None, ('rows', 'cols')), may hold values from 1 to 8
- normals: float32 [6, 4194304], P(None, ('rows', 'cols')), may hold values from -6 to 6
- position: float32 [3, 4194304], P(None, ('rows', 'cols')), may hold values from 2 to 6
- sh_coeffs: float32 [48, 4194304], P(None, ('rows', 'cols')), may hold values from -2 to 2
- camera: float32 [2, 3], replicated, may hold values from -1 to 1
- requests: int32 [128, 128, 256], P(('rows', 'cols')), may hold values from 0 to 32767
- tile_lists: int32 [2, 64, 64, 512], P(None, 'rows', 'cols'), may hold values from 0 to 32767
- list_lengths: int32 [2, 64, 64], P(None, 'rows', 'cols'), may hold values from 1 to 512, 13056 in all within a row
Outputs:
- image: float32 [2, 3, 1024, 1024], P(None, None, 'rows', 'cols')
- consistency: float32 [2, 1024, 1024], P(None, 'rows', 'cols')
The draws below stay inside these ranges and needn't reach their ends.
Inputs may be any that keep to these rules, and one draw needn't show every extreme that they name: `list_lengths`: in every tile row of each view the lengths sum to 13056, and the longest list of such a row holds exactly 512 slots.
All inputs are finite; a program needn't handle non-finite values. No bound on the sum of `list_lengths` on one device may be relied on, other than what follows from the above.
Results may differ from the reference program's by a relative error of at most 0.0003.
Values sent between devices are 32-bit elements; how exact they have to be, the bound alone decides.
A program may use at most 256 MiB of HBM per device.

```python
import math
import jax
import jax.numpy as jnp
import numpy as np
from jax import lax

VIEWS = 2
TR = 4
TC = 8
MAXLEN = 512
SH = 48
SURF_DEV = 32768
CAP = 256
SURFELS = 4194304
NTR = 64
NTC = 64
TOTAL_LEN = 13056
N_ROWS = 16
N_COLS = 8
DEVICES = 128


def with_ends(result, rng, least, largest):
    place = [jax.random.randint(jax.random.fold_in(rng, axis), (), 0, length) for axis, length in enumerate(result.shape)]
    longest = result.shape.index(max(result.shape))
    next_to = place[:longest] + [(place[longest] + 1) % result.shape[longest]] + place[longest + 1:]
    return result.at[tuple(place)].set(least).at[tuple(next_to)].set(largest)


def levels(stream_key, dims, cuts, smallest, largest):
    factor_of, own = 1.0, jax.random.fold_in(stream_key, 6)
    for dim, parts in cuts:
        draws = jnp.exp(jax.random.uniform(jax.random.fold_in(own, dim), (parts,), jnp.float32, smallest / len(cuts), largest / len(cuts)))
        factor_of = factor_of * jnp.repeat(draws, dims[dim] // parts).reshape([-1 if axis == dim else 1 for axis in range(len(dims))])
    return factor_of


def profile(number_of, total, bound, slope):
    portions = [(1 << 20) // math.isqrt(standing ** slope) + 1 for standing in range(2, number_of + 1)]
    spare, given = total - bound - (number_of - 1), [1] * (number_of - 1)
    while spare > 0:
        free = [i for i in range(number_of - 1) if given[i] < bound]
        mass, budget = sum([portions[i] for i in free]), spare
        for i in free:
            addition = min(bound - given[i], max(1, budget * portions[i] // mass), spare)
            given[i] = given[i] + addition
            spare = spare - addition
    return np.array([bound] + given)


def ragged_sizes(rng, amount, total, limit, slope):
    if amount == 2:
        one = jax.random.randint(rng, (), max(1, total - limit), min(limit, total - 1) + 1)
        return jnp.stack([one, total - one])
    tallies = jnp.asarray(profile(amount, total, limit, slope), jnp.int32)
    pairs = (amount - 1) // 2
    giver, receiver = tallies[1:1 + 2 * pairs:2], tallies[2:2 + 2 * pairs:2]
    slack = jnp.minimum(giver - 1, limit - receiver)
    shifted = jax.random.randint(jax.random.fold_in(rng, 1), (pairs,), 0, 1 << 20) % (slack + 1)
    tallies = tallies.at[1:1 + 2 * pairs:2].set(giver - shifted).at[2:2 + 2 * pairs:2].set(receiver + shifted)
    return tallies[jax.random.permutation(jax.random.fold_in(rng, 2), amount)]


def gaussian(rng, shape, spread, reach, shards=(), held_as=jnp.bfloat16):
    entries = spread * jax.random.normal(rng, shape, jnp.float32)
    if shards:
        entries = entries * levels(rng, shape, shards, -0.22, 0.18)
    return jnp.clip(entries, -reach, reach).astype(held_as)


def setup_inputs(seed: int = 0) -> dict:
    key_list = jax.random.split(jax.random.key(seed), 11)
    splat_map = gaussian(key_list[0], (6 * VIEWS, SURFELS), 2.0, 8.0, ((1, 128),), jnp.float32)
    opacity = jnp.clip(jnp.exp(math.log(0.2) - 3.6888795 * jax.random.uniform(key_list[1], (SURFELS,), jnp.float32) ** levels(key_list[1], (SURFELS,), ((0, 128),), -0.2, 0.2)), 0.005, 0.2)
    depths = jnp.clip(jnp.exp(math.log(8.0) - 2.0794415 * jax.random.uniform(key_list[2], (VIEWS, SURFELS), jnp.float32) ** levels(key_list[2], (VIEWS, SURFELS), ((1, 128),), -0.2, 0.2)), 1.0, 8.0)
    normals = gaussian(key_list[3], (3 * VIEWS, SURFELS), 1.0, 6.0, ((1, 128),), jnp.float32)
    position = jnp.clip(2.0 + 4.0 * jax.random.uniform(key_list[4], (3, SURFELS), jnp.float32) ** levels(key_list[4], (3, SURFELS), ((1, 128),), -0.2, 0.2), 2.0, 6.0)
    sh_coeffs = gaussian(key_list[5], (SH, SURFELS), 0.3, 2.0, ((1, 128),), jnp.float32)
    camera = jnp.clip(jax.random.uniform(key_list[6], (VIEWS, 3), jnp.float32, -1.0, 1.0), -1.0, 1.0)
    requests = with_ends(jax.random.randint(key_list[7], (DEVICES, DEVICES, CAP), 0, SURF_DEV), jax.random.fold_in(key_list[7], 1), 0, SURF_DEV - 1).astype(jnp.int32)
    tile_lists = with_ends(jax.random.randint(key_list[8], (VIEWS, NTR, NTC, MAXLEN), 0, DEVICES * CAP), jax.random.fold_in(key_list[8], 1), 0, (DEVICES * CAP) - 1).astype(jnp.int32)
    list_lengths = jax.vmap(lambda own: ragged_sizes(own, NTC, TOTAL_LEN, MAXLEN, 2))(jax.random.split(key_list[9], VIEWS * NTR)).reshape((VIEWS, NTR, NTC)).astype(jnp.int32)
    return dict(splat_map=splat_map, opacity=opacity, depths=depths, normals=normals, position=position, sh_coeffs=sh_coeffs, camera=camera, requests=requests, tile_lists=tile_lists, list_lengths=list_lengths)


sh_first = 0.28209479177387814
sh_second = 0.4886025119029199
sh_third = [1.0925484305920792, -1.0925484305920792, 0.31539156525252005, -1.0925484305920792, 0.5462742152960396]
sh_fourth = [-0.5900435899266435, 2.890611442640554, -0.4570457994644658, 0.3731763325901154, -0.4570457994644658, 1.445305721320277, -0.5900435899266435]

def shade(position, sh_coeffs, camera):
    offset = position[None, :, :] - camera[:, :, None]
    distance = jnp.sqrt(lax.optimization_barrier(jnp.sum(offset * offset, axis=1, keepdims=True)))
    direction = offset / distance
    dir_x = direction[:, 0]
    dir_y = direction[:, 1]
    dir_z = direction[:, 2]
    sq_x = dir_x * dir_x
    sq_y = dir_y * dir_y
    sq_z = dir_z * dir_z
    sh_basis = jnp.stack([jnp.full_like(dir_x, sh_first), -sh_second * dir_y, sh_second * dir_z, -sh_second * dir_x, sh_third[0] * dir_x * dir_y, sh_third[1] * dir_y * dir_z, sh_third[2] * (2.0 * sq_z - sq_x - sq_y), sh_third[3] * dir_x * dir_z, sh_third[4] * (sq_x - sq_y), sh_fourth[0] * dir_y * (3.0 * sq_x - sq_y), sh_fourth[1] * dir_x * dir_y * dir_z, sh_fourth[2] * dir_y * (4.0 * sq_z - sq_x - sq_y), sh_fourth[3] * dir_z * (2.0 * sq_z - 3.0 * sq_x - 3.0 * sq_y), sh_fourth[4] * dir_x * (4.0 * sq_z - sq_x - sq_y), sh_fourth[5] * dir_z * (sq_x - sq_y), sh_fourth[6] * dir_x * (sq_x - 3.0 * sq_y)], axis=1)
    coefficients = sh_coeffs.reshape(3, 16, -1)
    colour = 0.5 + lax.optimization_barrier(jnp.sum(sh_basis[:, None] * coefficients[None], axis=2))
    return jnp.maximum(colour, 0.0).reshape(-1, position.shape[1])

def render_device(field_table, slot_lists, lengths):
    view_count, tile_rows, tile_cols, slot_count = slot_lists.shape
    tile_count = tile_rows * tile_cols
    pixel_ids = jnp.arange(256, dtype=jnp.int32)
    local_x = ((pixel_ids % 16).astype(jnp.float32) - 7.5) / 8.0
    local_y = ((pixel_ids // 16).astype(jnp.float32) - 7.5) / 8.0
    positions = jnp.arange(slot_count, dtype=jnp.int32)
    rendered = []
    for view_index in range(view_count):
        slot_fields = jnp.take(field_table, slot_lists[view_index].reshape(-1), axis=1)
        slot_fields = slot_fields.reshape(field_table.shape[0], tile_count, slot_count)
        splat_rows = slot_fields[6 * view_index:6 * view_index + 6]
        opacities = slot_fields[6 * view_count]
        features = jnp.concatenate([slot_fields[10 * view_count + 1 + 3 * view_index:10 * view_count + 4 + 3 * view_index], slot_fields[6 * view_count + 1 + view_index:6 * view_count + 2 + view_index], slot_fields[7 * view_count + 1 + 3 * view_index:7 * view_count + 4 + 3 * view_index]], 0)
        live_mask = (positions[None, :] < lengths[view_index].reshape(-1, 1)).astype(jnp.float32)
        coord_u = splat_rows[0][:, None, :] * local_x[None, :, None] + splat_rows[1][:, None, :] * local_y[None, :, None] + splat_rows[2][:, None, :]
        coord_w = splat_rows[3][:, None, :] * local_x[None, :, None] + splat_rows[4][:, None, :] * local_y[None, :, None] + splat_rows[5][:, None, :]
        alphas = opacities[:, None, :] * jnp.exp(-0.5 * (coord_u * coord_u + coord_w * coord_w))
        log_keep = jnp.log1p(-alphas) * live_mask[:, None, :]
        before = jnp.cumsum(log_keep, axis=2) - log_keep
        weight = alphas * jnp.exp(before) * live_mask[:, None, :]
        totals = jnp.einsum('fts,tps->tfp', features, weight, precision=lax.Precision.HIGHEST)
        rendered.append(totals.reshape(tile_rows, tile_cols, 7, 16, 16).transpose(2, 0, 3, 1, 4).reshape(7, tile_rows * 16, tile_cols * 16))
    return jnp.stack(rendered)

def reference(splat_map, opacity, depths, normals, position, sh_coeffs, camera, requests, tile_lists, list_lengths):
    device_count = N_ROWS * N_COLS
    per_owner = opacity.shape[0] // device_count
    geometry = jnp.concatenate([splat_map, opacity[None, :], depths, normals], 0)
    lists_dev = tile_lists.reshape(VIEWS, N_ROWS, TR, N_COLS, TC, MAXLEN).transpose(1, 3, 0, 2, 4, 5).reshape(device_count, VIEWS, TR, TC, MAXLEN)
    lengths_dev = list_lengths.reshape(VIEWS, N_ROWS, TR, N_COLS, TC).transpose(1, 3, 0, 2, 4).reshape(device_count, VIEWS, TR, TC)
    owner_first = jnp.arange(device_count, dtype=jnp.int32)[:, None] * per_owner

    def render_one(operands):
        asked_for, slot_lists, lengths = operands
        source = (asked_for + owner_first).reshape(-1).astype(jnp.int32)
        field_table = jnp.concatenate([jnp.take(geometry, source, axis=1), shade(jnp.take(position, source, axis=1), jnp.take(sh_coeffs, source, axis=1), camera)], 0)
        return render_device(field_table, slot_lists, lengths)
    feature_maps = lax.map(render_one, (requests, lists_dev, lengths_dev))
    feature_maps = feature_maps.reshape(N_ROWS, N_COLS, VIEWS, 7, TR * 16, TC * 16).transpose(2, 3, 0, 4, 1, 5)
    feature_maps = feature_maps.reshape(VIEWS, 7, N_ROWS * TR * 16, N_COLS * TC * 16)
    image = feature_maps[:, :3]
    depth_map = feature_maps[:, 3]
    normal_map = feature_maps[:, 4:7]
    padded = jnp.pad(depth_map, ((0, 0), (1, 1), (1, 1)))
    grad_x = 0.5 * (padded[:, 1:-1, 2:] - padded[:, 1:-1, :-2])
    grad_y = 0.5 * (padded[:, 2:, 1:-1] - padded[:, :-2, 1:-1])
    inverse = 1.0 / jnp.sqrt(grad_x * grad_x + grad_y * grad_y + 1.0)
    consistency = 1.0 - (normal_map[:, 2] - normal_map[:, 0] * grad_x - normal_map[:, 1] * grad_y) * inverse
    return (image, consistency)
```

```python
import functools
import math

import jax
import jax.numpy as jnp
import numpy as np
from jax import lax
from jax.experimental import pallas as pl
from jax.experimental.pallas import tpu as pltpu
from jax.sharding import PartitionSpec as P

sh_first = 0.28209479177387814
sh_second = 0.4886025119029199
sh_third = [
    1.0925484305920792,
    -1.0925484305920792,
    0.31539156525252005,
    -1.0925484305920792,
    0.5462742152960396,
]
sh_fourth = [
    -0.5900435899266435,
    2.890611442640554,
    -0.4570457994644658,
    0.3731763325901154,
    -0.4570457994644658,
    1.445305721320277,
    -0.5900435899266435,
]
LOG2E = 1.4426950408889634
MIB = 1 << 20
IN_ROWS = 88
OUT_ROWS = 32
SHADE_BLOCK = 1024
ROWS = 24
LIMIT = 4 * ROWS


def dense_block(src, field):
    return src[pl.ds(field, 8, stride=IN_ROWS), :]


def shade_kernel(
    camera, splat, opacity, depths, normals, position, coeffs, table, fields_in, fields_out
):
    chunks = SHADE_BLOCK // 128
    for j in range(chunks):
        cols = slice(j * 128, (j + 1) * 128)
        first = j * IN_ROWS
        fields_in[first : first + 12, :] = splat[:, cols]
        fields_in[first + 16 : first + 18, :] = depths[:, cols]
        fields_in[first + 24 : first + 30, :] = normals[:, cols]
        fields_in[first + 32 : first + 35, :] = position[:, cols]
        fields_in[first + 40 : first + 88, :] = coeffs[:, cols]
    field = functools.partial(dense_block, fields_in)
    log_opacity = jnp.log(opacity[...]) * LOG2E
    zero = jnp.zeros((8, 128), jnp.float32)
    bases = []
    for view in range(2):

        def put(row, value, view=view):
            fields_out[pl.ds(16 * view + row, 8, stride=OUT_ROWS), :] = value

        m = [field(6 * view + k) for k in range(6)]
        half = -0.5 * LOG2E
        put(0, half * (m[0] * m[0] + m[3] * m[3]))
        put(1, (2.0 * half) * (m[0] * m[1] + m[3] * m[4]))
        put(2, half * (m[1] * m[1] + m[4] * m[4]))
        put(3, (2.0 * half) * (m[0] * m[2] + m[3] * m[5]))
        put(4, (2.0 * half) * (m[1] * m[2] + m[4] * m[5]))
        put(5, half * (m[2] * m[2] + m[5] * m[5]) + log_opacity)
        put(6, zero)
        put(7, zero)
        put(11, field(16 + view))
        for k in range(3):
            put(12 + k, field(24 + 3 * view + k))
        put(15, zero)
        off = [field(32 + k) - camera[view, k] for k in range(3)]
        distance = jnp.sqrt(off[0] * off[0] + off[1] * off[1] + off[2] * off[2])
        inverse = 1.0 / distance
        dir_x, dir_y, dir_z = [o * inverse for o in off]
        sq_x = dir_x * dir_x
        sq_y = dir_y * dir_y
        sq_z = dir_z * dir_z
        bases.append(
            [
                None,
                -sh_second * dir_y,
                sh_second * dir_z,
                -sh_second * dir_x,
                sh_third[0] * dir_x * dir_y,
                sh_third[1] * dir_y * dir_z,
                sh_third[2] * (2.0 * sq_z - sq_x - sq_y),
                sh_third[3] * dir_x * dir_z,
                sh_third[4] * (sq_x - sq_y),
                sh_fourth[0] * dir_y * (3.0 * sq_x - sq_y),
                sh_fourth[1] * dir_x * dir_y * dir_z,
                sh_fourth[2] * dir_y * (4.0 * sq_z - sq_x - sq_y),
                sh_fourth[3] * dir_z * (2.0 * sq_z - 3.0 * sq_x - 3.0 * sq_y),
                sh_fourth[4] * dir_x * (4.0 * sq_z - sq_x - sq_y),
                sh_fourth[5] * dir_z * (sq_x - sq_y),
                sh_fourth[6] * dir_x * (sq_x - 3.0 * sq_y),
            ]
        )
    for channel in range(3):
        c = field(40 + 16 * channel)
        sums = [0.5 + sh_first * c, 0.5 + sh_first * c]
        for k in range(1, 16):
            c = field(40 + 16 * channel + k)
            for view in range(2):
                sums[view] = sums[view] + bases[view][k] * c
        for view in range(2):
            fields_out[pl.ds(16 * view + 8 + channel, 8, stride=OUT_ROWS), :] = jnp.maximum(
                sums[view], 0.0
            )
    for j in range(chunks):
        first = fields_out[j * OUT_ROWS : j * OUT_ROWS + 16, :]
        second = fields_out[j * OUT_ROWS + 16 : j * OUT_ROWS + 32, :]
        block = jnp.concatenate([first] * 4 + [second] * 4, axis=0)
        table[j * 128 : (j + 1) * 128, :] = block.T


def shade_table(splat_map, opacity, depths, normals, position, sh_coeffs, camera):
    count = opacity.shape[0]
    dims = [12, 2, 6, 3, 48]

    def cols(rows):
        return pl.BlockSpec((rows, SHADE_BLOCK), lambda i: (0, i))

    return pl.pallas_call(
        shade_kernel,
        grid=(count // SHADE_BLOCK,),
        out_shape=jax.ShapeDtypeStruct((count, 128), jnp.float32),
        in_specs=[
            pl.BlockSpec(memory_space=pltpu.SMEM),
            cols(12),
            pl.BlockSpec((8, 128), lambda i: (i, 0)),
            cols(2),
            cols(6),
            cols(3),
            cols(48),
        ],
        out_specs=pl.BlockSpec((SHADE_BLOCK, 128), lambda i: (i, 0)),
        scratch_shapes=[
            pltpu.VMEM((8 * IN_ROWS, 128), jnp.float32),
            pltpu.VMEM((8 * OUT_ROWS, 128), jnp.float32),
        ],
        compiler_params=pltpu.CompilerParams(vmem_limit_bytes=32 * MIB),
        name="shade_table",
    )(camera, splat_map, opacity.reshape(-1, 128), depths, normals, position, sh_coeffs)


def plan_kernel(lengths, lists, requests, lower, message, places, used, packed):
    owner_row = lax.broadcasted_iota(jnp.int32, (128, 256), 0)
    entry_row = lax.broadcasted_iota(jnp.int32, (256, 256), 0)
    slot = lax.broadcasted_iota(jnp.int32, (1, 256), 1)
    wanted = requests[...].astype(jnp.float32).T
    packed[192:256, :] = jnp.zeros((64, 128), jnp.float32)
    most = jnp.zeros((1, 128), jnp.float32)
    for view in range(2):
        used[...] = jnp.zeros_like(used)

        def mark(tile, state, view=view):
            tile = 32 * view + tile
            length = lengths[tile]
            for part in range(2):

                @pl.when(length > 256 * part)
                def _():
                    place = lists[pl.ds(tile, 1), 256 * part : 256 * part + 256]
                    live = slot + 256 * part < length
                    owner = jnp.where(live, place // 256, -1)
                    is_owner = (owner_row == owner).astype(jnp.float32).astype(jnp.bfloat16)
                    is_entry = (entry_row == place % 256).astype(jnp.float32).astype(jnp.bfloat16)
                    used[...] += lax.dot_general(
                        is_entry,
                        is_owner,
                        (((1,), (1,)), ((), ())),
                        preferred_element_type=jnp.float32,
                    )

            return state

        lax.fori_loop(0, 32, mark, 0)
        flag = jnp.minimum(used[...], 1.0)
        rank = jnp.dot(lower[...], flag.astype(jnp.bfloat16), preferred_element_type=jnp.float32)
        most = jnp.maximum(most, rank[255:256] + flag[255:256])
        level = jnp.floor(rank * 0.25)
        owner = lax.broadcasted_iota(jnp.int32, (256, 128), 1).astype(jnp.float32)
        place = (rank - 4.0 * level + 4.0 * view) * (128.0 * ROWS) + owner * ROWS + level
        places[view] = place.T.astype(jnp.int32)
        rank = jnp.where(flag > 0.0, rank, -1.0)

        def pick(step, state, view=view, rank=rank):
            for i in range(8):
                entry = step * 8 + i
                chosen = jnp.where(rank == entry.astype(jnp.float32), wanted, 0.0)
                packed[pl.ds(view * LIMIT + entry, 1), :] = jnp.sum(chosen, axis=0, keepdims=True)
            return state

        lax.fori_loop(0, LIMIT // 8, pick, 0)
    over = (most > LIMIT).astype(jnp.float32)
    packed[255:256, :] = jnp.broadcast_to(jnp.max(over, axis=1, keepdims=True), (1, 128))
    message[...] = packed[...].T.astype(jnp.int32)


def plan(lengths, lists, requests):
    vmem = pl.BlockSpec(memory_space=pltpu.VMEM)
    index = np.arange(256)
    lower = jnp.asarray(index[None, :] < index[:, None], jnp.bfloat16)
    return pl.pallas_call(
        plan_kernel,
        out_shape=[
            jax.ShapeDtypeStruct((128, 256), jnp.int32),
            jax.ShapeDtypeStruct((2, 128, 256), jnp.int32),
        ],
        in_specs=[pl.BlockSpec(memory_space=pltpu.SMEM), vmem, vmem, vmem],
        out_specs=[vmem, vmem],
        scratch_shapes=[
            pltpu.VMEM((256, 128), jnp.float32),
            pltpu.VMEM((256, 128), jnp.float32),
        ],
        compiler_params=pltpu.CompilerParams(vmem_limit_bytes=32 * MIB),
        name="plan",
    )(lengths, lists, requests, lower)


def gather_kernel(wanted, table, out):
    group = lax.broadcasted_iota(jnp.int32, (1, 128), 1) // 16

    def body(step, state):
        dest = step // (ROWS // 8)
        base = dest * 256 + lax.rem(step, ROWS // 8) * 32
        for i in range(8):
            picked = [
                table[pl.ds(wanted[base + (g // 4) * LIMIT + 4 * i + g % 4], 1), :]
                for g in range(8)
            ]
            for bit in (1, 2, 4):
                picked = [
                    jnp.where((group // bit) % 2 == 0, picked[n], picked[n + 1])
                    for n in range(0, len(picked), 2)
                ]
            out[pl.ds(step * 8 + i, 1), :] = picked[0]
        return state

    lax.fori_loop(0, 128 * ROWS // 8, body, 0)


def gather_rows(wanted, table):
    return pl.pallas_call(
        gather_kernel,
        out_shape=jax.ShapeDtypeStruct((128 * ROWS, 128), jnp.float32),
        in_specs=[
            pl.BlockSpec(memory_space=pltpu.SMEM),
            pl.BlockSpec(memory_space=pltpu.VMEM),
        ],
        out_specs=pl.BlockSpec(memory_space=pltpu.VMEM),
        compiler_params=pltpu.CompilerParams(vmem_limit_bytes=40 * MIB),
        name="gather_rows",
    )(wanted, table)


def pixel_basis():
    pixel = np.arange(256)
    x = ((pixel % 16) - 7.5) / 8.0
    y = ((pixel // 16) - 7.5) / 8.0
    basis = np.zeros((128, 256), np.float32)
    for part in range(3):
        for k, value in enumerate([x * x, x * y, y * y, x, y, np.ones(256)]):
            basis[16 * part + k] = value
    return jnp.asarray(basis, jnp.bfloat16)


def prefix_matrix():
    slot = np.arange(128)
    earlier = (slot[None, :] < slot[:, None]).astype(np.float32)
    half = np.concatenate([earlier, np.ones((16, 128), np.float32)], axis=0)
    return jnp.asarray(np.concatenate([half, half], axis=1), jnp.bfloat16)


def swap_groups(block):
    row = lax.broadcasted_iota(jnp.int32, (8, 128), 0)
    group = lax.broadcasted_iota(jnp.int32, (8, 128), 1) // 16
    for bit in (1, 2, 4):
        row_bit = (row // bit) % 2
        group_bit = (group // bit) % 2
        from_below = pltpu.roll(pltpu.roll(block, 8 - bit, 0), 16 * bit, 1)
        from_above = pltpu.roll(pltpu.roll(block, bit, 0), 128 - 16 * bit, 1)
        block = jnp.where(
            row_bit == group_bit, block, jnp.where(row_bit < group_bit, from_below, from_above)
        )
    return block


def render_kernel(
    counts, slots, places, packed, basis, prefix, image, maps, table, picked, totals, carry, stage,
    closed, alphas_of, keep_of, weight_of, turned_of
):
    packed_rows = packed.shape[0]
    lane = lax.broadcasted_iota(jnp.int32, (8, 128), 1)
    group = lane // 16

    def unpack(step, state):
        base = pl.multiple_of(step * 8, 8)
        whole = packed[pl.ds(base, 8), :]
        high = whole.astype(jnp.bfloat16).astype(jnp.float32)
        rest = whole - high
        mid = rest.astype(jnp.bfloat16).astype(jnp.float32)
        low = pltpu.roll(rest - mid, 32, 1)
        mid = pltpu.roll(mid, 16, 1)
        for g in range(8):
            row = jnp.where(group == g, high, jnp.where(group == (g + 1) % 8, mid, low))
            if g:
                row = pltpu.roll(row, 128 - 16 * g, 1)
            table[pl.ds(pl.multiple_of(g * packed_rows + base, 8), 8), :] = row
        return state

    lax.fori_loop(0, packed_rows // 8, unpack, 0, unroll=16)
    table[8 * packed_rows : 8 * packed_rows + 8, :] = jnp.where(lane == 5, -300.0, 0.0)
    def gather(place, spot):
        first = spot[0] * 512 + spot[1] * 128
        for i in range(128):
            picked[place + i : place + i + 1, :] = table[pl.ds(places[slots[first + i]], 1), :]

    def finish(tile, result):
        column = lax.rem(tile, 8)
        for h in range(2):
            stage[pl.ds(h * 8 + column, 8, stride=16), :] = result[:, h * 128 : (h + 1) * 128]

        @pl.when(column == 7)
        def _():
            view = tile // 32
            tile_row = lax.rem(tile // 8, 4)
            for f in range(7):
                for h in range(2):
                    block = swap_groups(stage[(2 * f + h) * 8 : (2 * f + h) * 8 + 8, :])
                    place = pl.ds(pl.multiple_of(tile_row * 16 + h * 8, 8), 8)
                    if f < 3:
                        image[view, f, place, :] = block
                    else:
                        maps[view, f - 3, place, :] = block

    totals[...] = jnp.zeros_like(totals)
    carry[...] = jnp.zeros_like(carry)
    alphas_of[...] = jnp.zeros_like(alphas_of)
    keep_of[...] = jnp.zeros_like(keep_of)
    weight_of[...] = jnp.zeros_like(weight_of)
    turned_of[...] = jnp.zeros_like(turned_of)

    def following(spot):
        tile, block, last = spot
        next_tile = jnp.where(last == 1, jnp.minimum(tile + 1, 63), tile)
        next_block = jnp.where(last == 1, 0, block + 1)
        return with_last(next_tile, next_block)

    def with_last(tile, block):
        return tile, block, (block + 1 >= counts[tile]).astype(jnp.int32)

    start = with_last(jnp.int32(0), jnp.int32(0))
    second = following(start)
    gather(0, start)
    gather(128, second)

    def split(value):
        high = value.astype(jnp.bfloat16)
        return high, (value - high.astype(jnp.float32)).astype(jnp.bfloat16)

    def step(index, state):
        now, ago, old = state
        later = following(now[1])
        later = (later, following(later))

        parts = []
        for n in range(2):
            part = jnp.dot(
                jnp.concatenate([turned_of[1, n]] * 2, axis=1),
                weight_of[n],
                preferred_element_type=jnp.float32,
            )
            parts.append(part[:8] + part[8:16] + part[16:24])
        first_done = totals[...] + parts[0]
        closed[...] = first_done
        totals[...] = first_done * (1 - old[0][2]).astype(jnp.float32) + parts[1]

        before = carry[...]
        for n in range(2):
            fresh = (ago[n][1] == 0).astype(jnp.int32)
            before = before * (1 - fresh).astype(jnp.float32)
            sums = jnp.dot(prefix[...], keep_of[n], preferred_element_type=jnp.float32)
            ahead = sums[:128] + jnp.concatenate([before] * 16, axis=0)
            high, low = split(alphas_of[n] * jnp.exp(ahead))
            before = before + sums[128:136]
            weight_of[n, :128, :] = high
            weight_of[n, 128:, :] = low
        carry[...] = before

        turned_of[1] = turned_of[0]
        for n in range(2):
            rows = picked[128 * n : 128 * n + 128, :]
            turned = rows.T
            turned_of[0, n] = jnp.concatenate(
                [turned[8:16], turned[24:32], turned[40:48], turned[40:48]], axis=0
            ).astype(jnp.bfloat16)
            power = jnp.dot(
                rows.astype(jnp.bfloat16), basis[...], preferred_element_type=jnp.float32
            )
            alphas = jnp.exp2(power)
            alphas_of[n] = alphas
            high, low = split(jnp.log(1.0 - alphas))
            keep_of[n, :128, :] = high
            keep_of[n, 128:, :] = low
        for n in range(2):
            gather(128 * n, later[n])

        @pl.when(old[0][2] == 1)
        def _():
            finish(old[0][0], closed)

        @pl.when(old[1][2] == 1)
        def _():
            finish(old[1][0], totals)
            totals[...] = jnp.zeros_like(totals)

        return later, now, ago

    steps = lax.fori_loop(0, 64, lambda i, n: n + counts[i], 0)
    zero = jnp.int32(0)
    none = ((zero, zero, zero), (zero, zero, zero))
    lax.fori_loop(0, (steps + 1) // 2 + 2, step, ((start, second), none, none))


def render(counts, slots, places, packed):
    packed_rows = packed.shape[0]
    vmem = pl.BlockSpec(memory_space=pltpu.VMEM)
    smem = pl.BlockSpec(memory_space=pltpu.SMEM)
    return pl.pallas_call(
        render_kernel,
        out_shape=[
            jax.ShapeDtypeStruct((2, 3, 64, 128), jnp.float32),
            jax.ShapeDtypeStruct((2, 4, 64, 128), jnp.float32),
        ],
        in_specs=[smem, smem, smem, vmem, vmem, vmem],
        out_specs=[vmem, vmem],
        scratch_shapes=[
            pltpu.VMEM((8 * packed_rows + 8, 128), jnp.float32),
            pltpu.VMEM((256, 128), jnp.float32),
            pltpu.VMEM((8, 256), jnp.float32),
            pltpu.VMEM((8, 256), jnp.float32),
            pltpu.VMEM((128, 128), jnp.float32),
            pltpu.VMEM((8, 256), jnp.float32),
            pltpu.VMEM((2, 128, 256), jnp.float32),
            pltpu.VMEM((2, 256, 256), jnp.bfloat16),
            pltpu.VMEM((2, 256, 256), jnp.bfloat16),
            pltpu.VMEM((2, 2, 32, 128), jnp.bfloat16),
        ],
        compiler_params=pltpu.CompilerParams(vmem_limit_bytes=52 * MIB),
        name="render",
    )(counts, slots, places, packed, pixel_basis(), prefix_matrix())


def shift(edge, axis, step):
    count = lax.axis_size(axis)
    pairs = [(i, i + step) for i in range(count) if 0 <= i + step < count]
    return lax.ppermute(edge, axis, pairs)


def consistency_map(depth, normal):
    above = shift(depth[:, -1:, :], "rows", 1)
    below = shift(depth[:, :1, :], "rows", -1)
    before = shift(depth[:, :, -1:], "cols", 1)
    after = shift(depth[:, :, :1], "cols", -1)
    tall = jnp.concatenate([above, depth, below], axis=1)
    wide = jnp.concatenate([before, depth, after], axis=2)
    grad_x = 0.5 * (wide[:, :, 2:] - wide[:, :, :-2])
    grad_y = 0.5 * (tall[:, 2:] - tall[:, :-2])
    inverse = 1.0 / jnp.sqrt(grad_x * grad_x + grad_y * grad_y + 1.0)
    return 1.0 - (normal[:, 2] - normal[:, 0] * grad_x - normal[:, 1] * grad_y) * inverse


def shade(position, sh_coeffs, camera):
    offset = position[None, :, :] - camera[:, :, None]
    distance = jnp.sqrt(jnp.sum(offset * offset, axis=1, keepdims=True))
    direction = offset / distance
    dir_x = direction[:, 0]
    dir_y = direction[:, 1]
    dir_z = direction[:, 2]
    sq_x = dir_x * dir_x
    sq_y = dir_y * dir_y
    sq_z = dir_z * dir_z
    sh_basis = jnp.stack(
        [
            jnp.full_like(dir_x, sh_first),
            -sh_second * dir_y,
            sh_second * dir_z,
            -sh_second * dir_x,
            sh_third[0] * dir_x * dir_y,
            sh_third[1] * dir_y * dir_z,
            sh_third[2] * (2.0 * sq_z - sq_x - sq_y),
            sh_third[3] * dir_x * dir_z,
            sh_third[4] * (sq_x - sq_y),
            sh_fourth[0] * dir_y * (3.0 * sq_x - sq_y),
            sh_fourth[1] * dir_x * dir_y * dir_z,
            sh_fourth[2] * dir_y * (4.0 * sq_z - sq_x - sq_y),
            sh_fourth[3] * dir_z * (2.0 * sq_z - 3.0 * sq_x - 3.0 * sq_y),
            sh_fourth[4] * dir_x * (4.0 * sq_z - sq_x - sq_y),
            sh_fourth[5] * dir_z * (sq_x - sq_y),
            sh_fourth[6] * dir_x * (sq_x - 3.0 * sq_y),
        ],
        axis=1,
    )
    coefficients = sh_coeffs.reshape(3, 16, -1)
    colour = 0.5 + jnp.sum(sh_basis[:, None] * coefficients[None], axis=2)
    return jnp.maximum(colour, 0.0).reshape(-1, position.shape[1])


def composite(table_rows, slot_lists, lengths, view_index, view_count, block_count, block_size):
    tile_rows, tile_cols, slot_count = slot_lists.shape
    tile_count = tile_rows * tile_cols
    slot_index = slot_lists.reshape(tile_count, slot_count)
    live_count = lengths.reshape(tile_count)
    pixel_ids = jnp.arange(256, dtype=jnp.int32)
    local_x = ((pixel_ids % 16).astype(jnp.float32) - 7.5) / 8.0
    local_y = ((pixel_ids // 16).astype(jnp.float32) - 7.5) / 8.0
    positions = jnp.arange(block_size, dtype=jnp.int32)
    earlier = (positions[:, None] < positions[None, :]).astype(jnp.float32)
    feature_rows = (
        [10 * view_count + 1 + 3 * view_index + k for k in range(3)]
        + [6 * view_count + 1 + view_index]
        + [7 * view_count + 1 + 3 * view_index + k for k in range(3)]
    )

    def block_step(block_index, state):
        totals, log_before = state
        first_slot = block_index * block_size
        picked_index = lax.dynamic_slice_in_dim(slot_index, first_slot, block_size, 1)
        picked = jnp.take(table_rows, picked_index.reshape(-1), axis=0)
        picked = picked.reshape(tile_count, block_size, table_rows.shape[1]).transpose(2, 0, 1)
        part_map = picked[6 * view_index : 6 * view_index + 6]
        part_opacity = picked[6 * view_count]
        part_features = jnp.stack([picked[row] for row in feature_rows], 0)
        live_mask = ((first_slot + positions)[None, :] < live_count[:, None]).astype(jnp.float32)
        coord_u = (
            part_map[0][:, None, :] * local_x[None, :, None]
            + part_map[1][:, None, :] * local_y[None, :, None]
            + part_map[2][:, None, :]
        )
        coord_w = (
            part_map[3][:, None, :] * local_x[None, :, None]
            + part_map[4][:, None, :] * local_y[None, :, None]
            + part_map[5][:, None, :]
        )
        alphas = part_opacity[:, None, :] * jnp.exp(-0.5 * (coord_u * coord_u + coord_w * coord_w))
        log_keep = jnp.log1p(-alphas) * live_mask[:, None, :]
        before = log_before[:, :, None] + jnp.einsum(
            "tps,sq->tpq", log_keep, earlier, precision=lax.Precision.HIGHEST
        )
        weight = alphas * jnp.exp(before) * live_mask[:, None, :]
        totals = totals + jnp.einsum(
            "fts,tps->tfp", part_features, weight, precision=lax.Precision.HIGHEST
        )
        return (totals, log_before + jnp.sum(log_keep, axis=2))

    start_state = (
        jnp.zeros((tile_count, 7, 256), jnp.float32),
        jnp.zeros((tile_count, 256), jnp.float32),
    )
    totals, unused_log = lax.fori_loop(0, block_count, block_step, start_state)
    return (
        totals.reshape(tile_rows, tile_cols, 7, 16, 16)
        .transpose(2, 0, 3, 1, 4)
        .reshape(7, tile_rows * 16, tile_cols * 16)
    )


def general(
    splat_map,
    opacity,
    depths,
    normals,
    position,
    sh_coeffs,
    camera,
    requests,
    tile_lists,
    list_lengths,
):
    view_count = camera.shape[0]
    device_count = requests.shape[1]
    capacity = requests.shape[2]
    asked_for = lax.all_to_all(requests, ("rows", "cols"), split_axis=1, concat_axis=0, tiled=True)
    wanted = asked_for.reshape(-1)
    geometry_count = 10 * view_count + 1
    source_table = jnp.concatenate(
        [splat_map, opacity[None, :], depths, normals, position, sh_coeffs], 0
    ).T
    gathered = jnp.take(source_table, wanted, axis=0).T
    outgoing = jnp.concatenate(
        [
            gathered[:geometry_count],
            shade(
                gathered[geometry_count : geometry_count + 3],
                gathered[geometry_count + 3 :],
                camera,
            ),
        ],
        0,
    )
    field_rows = outgoing.shape[0]
    arrived = lax.all_to_all(
        outgoing.reshape(field_rows, device_count, capacity),
        ("rows", "cols"),
        split_axis=1,
        concat_axis=1,
        tiled=True,
    ).reshape(field_rows, device_count * capacity)
    padded_count = (field_rows + 7) // 8 * 8
    table_rows = jnp.pad(arrived, ((0, padded_count - field_rows), (0, 0))).T
    slot_count = tile_lists.shape[-1]
    block_size = min(128, slot_count)
    feature_maps = jnp.stack(
        [
            composite(
                table_rows,
                tile_lists[view_index],
                list_lengths[view_index],
                view_index,
                view_count,
                slot_count // block_size,
                block_size,
            )
            for view_index in range(view_count)
        ]
    )
    return feature_maps[:, :3], feature_maps[:, 3:]


def shards(
    splat_map,
    opacity,
    depths,
    normals,
    position,
    sh_coeffs,
    camera,
    requests,
    tile_lists,
    list_lengths,
):
    lengths = list_lengths.reshape(-1)
    message, places = plan(lengths, tile_lists.reshape(64, 512), requests[0])
    asked_for = lax.all_to_all(message, ("rows", "cols"), split_axis=0, concat_axis=0, tiled=True)
    table = shade_table(splat_map, opacity, depths, normals, position, sh_coeffs, camera)

    def fast():
        outgoing = gather_rows(asked_for.reshape(-1), table)
        arrived = lax.all_to_all(
            outgoing.reshape(128, ROWS, 128),
            ("rows", "cols"),
            split_axis=0,
            concat_axis=0,
            tiled=True,
        ).reshape(128 * ROWS, 128)
        slot = jnp.arange(512, dtype=jnp.int32)
        view = jnp.arange(2, dtype=jnp.int32)[:, None, None, None]
        slots = jnp.where(slot < list_lengths[..., None], tile_lists + 32768 * view, 65536)
        dead = jnp.full((8,), 8 * 128 * ROWS, jnp.int32)
        return render(
            (lengths + 127) // 128,
            slots.reshape(-1),
            jnp.concatenate([places.reshape(-1), dead]),
            arrived,
        )

    def slow():
        return general(
            splat_map,
            opacity,
            depths,
            normals,
            position,
            sh_coeffs,
            camera,
            requests,
            tile_lists,
            list_lengths,
        )

    image, maps = lax.cond(jnp.max(asked_for[:, 255]) > 0, slow, fast)
    return (image, consistency_map(maps[:, 0], maps[:, 1:]))


def solution(mesh):
    in_specs = (
        P(None, ("rows", "cols")),
        P(("rows", "cols")),
        P(None, ("rows", "cols")),
        P(None, ("rows", "cols")),
        P(None, ("rows", "cols")),
        P(None, ("rows", "cols")),
        P(),
        P(("rows", "cols"), None, None),
        P(None, "rows", "cols", None),
        P(None, "rows", "cols"),
    )
    out_specs = (P(None, None, "rows", "cols"), P(None, "rows", "cols"))
    return jax.shard_map(shards, mesh=mesh, in_specs=in_specs, out_specs=out_specs, check_vma=False)
```

```python
import functools
import math

import jax
import jax.numpy as jnp
import numpy as np
from jax import lax
from jax.experimental import pallas as pl
from jax.experimental.pallas import tpu as pltpu
from jax.sharding import PartitionSpec as P

sh_first = 0.28209479177387814
sh_second = 0.4886025119029199
sh_third = [
    1.0925484305920792,
    -1.0925484305920792,
    0.31539156525252005,
    -1.0925484305920792,
    0.5462742152960396,
]
sh_fourth = [
    -0.5900435899266435,
    2.890611442640554,
    -0.4570457994644658,
    0.3731763325901154,
    -0.4570457994644658,
    1.445305721320277,
    -0.5900435899266435,
]
LOG2E = 1.4426950408889634
MIB = 1 << 20
IN_ROWS = 88
OUT_ROWS = 32
SHADE_BLOCK = 4096
ROWS = 24
LIMIT = 4 * ROWS


def dense_block(src, field):
    return src[pl.ds(field, 8, stride=IN_ROWS), :]


def owner_kernel(
    camera,
    wanted,
    splat,
    opacity,
    depths,
    normals,
    position,
    coeffs,
    out,
    table,
    fields_in,
    fields_out,
):
    first_row = pl.program_id(0) * SHADE_BLOCK

    def shade_part(part, fields_in, fields_out):
        for j in range(8):
            cols = pl.ds(pl.multiple_of(part * 1024 + j * 128, 128), 128)
            first = j * IN_ROWS
            fields_in[first : first + 12, :] = splat[:, cols]
            fields_in[first + 16 : first + 18, :] = depths[:, cols]
            fields_in[first + 24 : first + 30, :] = normals[:, cols]
            fields_in[first + 32 : first + 35, :] = position[:, cols]
            fields_in[first + 40 : first + 88, :] = coeffs[:, cols]
        field = functools.partial(dense_block, fields_in)
        log_opacity = jnp.log(opacity[pl.ds(pl.multiple_of(part * 8, 8), 8), :]) * LOG2E
        zero = jnp.zeros((8, 128), jnp.float32)
        bases = []
        for view in range(2):

            def put(row, value, view=view):
                fields_out[pl.ds(16 * view + row, 8, stride=OUT_ROWS), :] = value

            m = [field(6 * view + k) for k in range(6)]
            half = -0.5 * LOG2E
            put(0, half * (m[0] * m[0] + m[3] * m[3]))
            put(1, (2.0 * half) * (m[0] * m[1] + m[3] * m[4]))
            put(2, half * (m[1] * m[1] + m[4] * m[4]))
            put(3, (2.0 * half) * (m[0] * m[2] + m[3] * m[5]))
            put(4, (2.0 * half) * (m[1] * m[2] + m[4] * m[5]))
            put(5, half * (m[2] * m[2] + m[5] * m[5]) + log_opacity)
            put(6, zero)
            put(7, zero)
            put(11, field(16 + view))
            for k in range(3):
                put(12 + k, field(24 + 3 * view + k))
            put(15, zero)
            off = [field(32 + k) - camera[view, k] for k in range(3)]
            distance = jnp.sqrt(off[0] * off[0] + off[1] * off[1] + off[2] * off[2])
            inverse = 1.0 / distance
            dir_x, dir_y, dir_z = [o * inverse for o in off]
            sq_x = dir_x * dir_x
            sq_y = dir_y * dir_y
            sq_z = dir_z * dir_z
            bases.append(
                [
                    None,
                    -sh_second * dir_y,
                    sh_second * dir_z,
                    -sh_second * dir_x,
                    sh_third[0] * dir_x * dir_y,
                    sh_third[1] * dir_y * dir_z,
                    sh_third[2] * (2.0 * sq_z - sq_x - sq_y),
                    sh_third[3] * dir_x * dir_z,
                    sh_third[4] * (sq_x - sq_y),
                    sh_fourth[0] * dir_y * (3.0 * sq_x - sq_y),
                    sh_fourth[1] * dir_x * dir_y * dir_z,
                    sh_fourth[2] * dir_y * (4.0 * sq_z - sq_x - sq_y),
                    sh_fourth[3] * dir_z * (2.0 * sq_z - 3.0 * sq_x - 3.0 * sq_y),
                    sh_fourth[4] * dir_x * (4.0 * sq_z - sq_x - sq_y),
                    sh_fourth[5] * dir_z * (sq_x - sq_y),
                    sh_fourth[6] * dir_x * (sq_x - 3.0 * sq_y),
                ]
            )
        for channel in range(3):
            c = field(40 + 16 * channel)
            sums = [0.5 + sh_first * c, 0.5 + sh_first * c]
            for k in range(1, 16):
                c = field(40 + 16 * channel + k)
                for view in range(2):
                    sums[view] = sums[view] + bases[view][k] * c
            for view in range(2):
                fields_out[pl.ds(16 * view + 8 + channel, 8, stride=OUT_ROWS), :] = jnp.maximum(
                    sums[view], 0.0
                )
        for j in range(8):
            first = fields_out[j * OUT_ROWS : j * OUT_ROWS + 16, :]
            second = fields_out[j * OUT_ROWS + 16 : j * OUT_ROWS + 32, :]
            block = jnp.concatenate([first] * 4 + [second] * 4, axis=0)
            table[pl.ds(pl.multiple_of(first_row + part * 1024 + j * 128, 128), 128), :] = block.T

    for part in range(SHADE_BLOCK // 1024):
        shade_part(part, fields_in.at[part], fields_out.at[part])

    @pl.when(pl.program_id(0) == pl.num_programs(0) - 1)
    def _():
        gather(wanted, table, out)


def gather(wanted, table, out):
    group = lax.broadcasted_iota(jnp.int32, (1, 128), 1) // 16

    def body(dest, state):
        count = jnp.maximum(wanted[dest * 256 + 253], wanted[dest * 256 + 254])

        def eight(step, state):
            base = dest * 256 + step * 32
            for i in range(8):
                picked = [
                    table[pl.ds(wanted[base + (g // 4) * LIMIT + 4 * i + g % 4], 1), :]
                    for g in range(8)
                ]
                for bit in (1, 2, 4):
                    picked = [
                        jnp.where((group // bit) % 2 == 0, picked[n], picked[n + 1])
                        for n in range(0, len(picked), 2)
                    ]
                out[pl.ds(dest * ROWS + step * 8 + i, 1), :] = picked[0]
            return state

        return lax.fori_loop(0, jnp.minimum((count + 31) // 32, ROWS // 8), eight, state)

    out[...] = jnp.zeros_like(out)
    lax.fori_loop(0, 128, body, 0)


def serve(wanted, splat_map, opacity, depths, normals, position, sh_coeffs, camera):
    count = opacity.shape[0]

    def cols(rows):
        return pl.BlockSpec((rows, SHADE_BLOCK), lambda i: (0, i))

    return pl.pallas_call(
        owner_kernel,
        grid=(count // SHADE_BLOCK,),
        out_shape=jax.ShapeDtypeStruct((128 * ROWS, 128), jnp.float32),
        in_specs=[
            pl.BlockSpec(memory_space=pltpu.SMEM),
            pl.BlockSpec(memory_space=pltpu.SMEM),
            cols(12),
            pl.BlockSpec((SHADE_BLOCK // 128, 128), lambda i: (i, 0)),
            cols(2),
            cols(6),
            cols(3),
            cols(48),
        ],
        out_specs=pl.BlockSpec(memory_space=pltpu.VMEM),
        scratch_shapes=[
            pltpu.VMEM((count, 128), jnp.float32),
            pltpu.VMEM((SHADE_BLOCK // 1024, 8 * IN_ROWS, 128), jnp.float32),
            pltpu.VMEM((SHADE_BLOCK // 1024, 8 * OUT_ROWS, 128), jnp.float32),
        ],
        compiler_params=pltpu.CompilerParams(vmem_limit_bytes=48 * MIB),
        name="serve",
    )(camera, wanted, splat_map, opacity.reshape(-1, 128), depths, normals, position, sh_coeffs)


def plan_kernel(lengths, lists, requests, lower, message, places, used, packed, owners, entries):
    owner_row = lax.broadcasted_iota(jnp.int32, (128, 512), 0)
    entry_row = lax.broadcasted_iota(jnp.int32, (256, 512), 0)
    slot = lax.broadcasted_iota(jnp.int32, (1, 128), 1)
    wanted = requests[...].astype(jnp.float32).T
    packed[192:256, :] = jnp.zeros((64, 128), jnp.float32)
    most = jnp.zeros((1, 128), jnp.float32)
    for view in range(2):
        used[...] = jnp.zeros_like(used)
        owners[...] = jnp.zeros_like(owners)
        entries[...] = jnp.zeros_like(entries)
        last_tile = 32 * view + 31

        def mark(step, spots):
            used[...] += lax.dot_general(
                entries[...],
                owners[...],
                (((1,), (1,)), ((), ())),
                preferred_element_type=jnp.float32,
            )
            tile, block = spots
            owner, entry = [], []
            for _ in range(4):
                row = jnp.minimum(tile, last_tile)
                first = block * 128
                place = lists[pl.ds(row * 4 + block, 1), :]
                length = jnp.where(tile > last_tile, 0, lengths[row])
                owner.append(jnp.where(slot + first < length, place // 256, -1))
                entry.append(place % 256)
                over = first + 128 >= length
                tile = jnp.where(over, tile + 1, tile)
                block = jnp.where(over, 0, block + 1)
            owner = jnp.concatenate(owner, axis=1)
            entry = jnp.concatenate(entry, axis=1)
            owners[...] = (owner_row == owner).astype(jnp.float32).astype(jnp.bfloat16)
            entries[...] = (entry_row == entry).astype(jnp.float32).astype(jnp.bfloat16)
            return tile, block

        blocks = lax.fori_loop(
            32 * view, 32 * view + 32, lambda t, n: n + (lengths[t] + 127) // 128, 0
        )
        lax.fori_loop(
            0, (blocks + 3) // 4 + 1, mark, (jnp.int32(32 * view), jnp.int32(0))
        )
        flag = jnp.minimum(used[...], 1.0)
        rank = jnp.dot(lower[...], flag.astype(jnp.bfloat16), preferred_element_type=jnp.float32)
        count = rank[255:256] + flag[255:256]
        packed[253 + view : 254 + view, :] = count
        most = jnp.maximum(most, count)
        level = jnp.floor(rank * 0.25)
        owner = lax.broadcasted_iota(jnp.int32, (256, 128), 1).astype(jnp.float32)
        place = (rank - 4.0 * level + 4.0 * view) * (128.0 * ROWS) + owner * ROWS + level
        places[view] = place.T.astype(jnp.int32)
        rank = jnp.where(flag > 0.0, rank, -1.0)

        def pick(step, state, view=view, rank=rank):
            for i in range(8):
                entry = step * 8 + i
                chosen = jnp.where(rank == entry.astype(jnp.float32), wanted, 0.0)
                packed[pl.ds(view * LIMIT + entry, 1), :] = jnp.sum(chosen, axis=0, keepdims=True)
            return state

        lax.fori_loop(0, LIMIT // 8, pick, 0)
    over = (most > LIMIT).astype(jnp.float32)
    packed[255:256, :] = jnp.broadcast_to(jnp.max(over, axis=1, keepdims=True), (1, 128))
    message[...] = packed[...].T.astype(jnp.int32)


def plan(lengths, lists, requests):
    vmem = pl.BlockSpec(memory_space=pltpu.VMEM)
    index = np.arange(256)
    lower = jnp.asarray(index[None, :] < index[:, None], jnp.bfloat16)
    return pl.pallas_call(
        plan_kernel,
        out_shape=[
            jax.ShapeDtypeStruct((128, 256), jnp.int32),
            jax.ShapeDtypeStruct((2, 128, 256), jnp.int32),
        ],
        in_specs=[pl.BlockSpec(memory_space=pltpu.SMEM), vmem, vmem, vmem],
        out_specs=[vmem, vmem],
        scratch_shapes=[
            pltpu.VMEM((256, 128), jnp.float32),
            pltpu.VMEM((256, 128), jnp.float32),
            pltpu.VMEM((128, 512), jnp.bfloat16),
            pltpu.VMEM((256, 512), jnp.bfloat16),
        ],
        compiler_params=pltpu.CompilerParams(vmem_limit_bytes=32 * MIB),
        name="plan",
    )(lengths, lists, requests, lower)


def pixel_basis():
    pixel = np.arange(256)
    x = ((pixel % 16) - 7.5) / 8.0
    y = ((pixel // 16) - 7.5) / 8.0
    basis = np.zeros((128, 256), np.float32)
    for part in range(3):
        for k, value in enumerate([x * x, x * y, y * y, x, y, np.ones(256)]):
            basis[16 * part + k] = value
    return jnp.asarray(basis, jnp.bfloat16)


def swap_groups(block):
    row = lax.broadcasted_iota(jnp.int32, (8, 128), 0)
    group = lax.broadcasted_iota(jnp.int32, (8, 128), 1) // 16
    for bit in (1, 2, 4):
        row_bit = (row // bit) % 2
        group_bit = (group // bit) % 2
        from_below = pltpu.roll(pltpu.roll(block, 8 - bit, 0), 16 * bit, 1)
        from_above = pltpu.roll(pltpu.roll(block, bit, 0), 128 - 16 * bit, 1)
        block = jnp.where(
            row_bit == group_bit, block, jnp.where(row_bit < group_bit, from_below, from_above)
        )
    return block


def render_kernel(
    counts, slots_in, places_in, packed, basis, image, maps, table, picked, totals, carry, stage,
    closed, alphas_of, weight_of, turned_of,
    slots, places, copy_sem
):
    copies = [
        pltpu.make_async_copy(slots_in, slots, copy_sem.at[0]),
        pltpu.make_async_copy(places_in, places, copy_sem.at[1]),
    ]
    for copy in copies:
        copy.start()
    packed_rows = packed.shape[0]
    lane = lax.broadcasted_iota(jnp.int32, (8, 128), 1)
    group = lane // 16

    def unpack(step, state):
        base = pl.multiple_of(step * 8, 8)
        whole = packed[pl.ds(base, 8), :]
        high = whole.astype(jnp.bfloat16).astype(jnp.float32)
        rest = whole - high
        mid = rest.astype(jnp.bfloat16).astype(jnp.float32)
        low = pltpu.roll(rest - mid, 32, 1)
        mid = pltpu.roll(mid, 16, 1)
        for g in range(8):
            row = jnp.where(group == g, high, jnp.where(group == (g + 1) % 8, mid, low))
            if g:
                row = pltpu.roll(row, 128 - 16 * g, 1)
            table[pl.ds(pl.multiple_of(g * packed_rows + base, 8), 8), :] = row
        return state

    lax.fori_loop(0, packed_rows // 8, unpack, 0, unroll=16)
    table[8 * packed_rows : 8 * packed_rows + 8, :] = jnp.where(lane == 5, -300.0, 0.0)
    def gather(place, spot):
        first = spot[0] * 512 + spot[1] * 128
        for i in range(128):
            slot = first + 16 * (i % 8) + i // 8
            picked[place + i : place + i + 1, :] = table[pl.ds(places[slots[slot]], 1), :]

    def finish(tile, result):
        column = lax.rem(tile, 8)
        for h in range(2):
            stage[pl.ds(h * 8 + column, 8, stride=16), :] = result[:, h * 128 : (h + 1) * 128]

        @pl.when(column == 7)
        def _():
            view = tile // 32
            tile_row = lax.rem(tile // 8, 4)
            for f in range(7):
                for h in range(2):
                    block = swap_groups(stage[(2 * f + h) * 8 : (2 * f + h) * 8 + 8, :])
                    place = pl.ds(pl.multiple_of(tile_row * 16 + h * 8, 8), 8)
                    if f < 3:
                        image[view, f, place, :] = block
                    else:
                        maps[view, f - 3, place, :] = block

    totals[...] = jnp.zeros_like(totals)
    carry[...] = jnp.ones_like(carry)
    alphas_of[...] = jnp.zeros_like(alphas_of)
    weight_of[...] = jnp.zeros_like(weight_of)
    turned_of[...] = jnp.zeros_like(turned_of)

    def following(spot):
        tile, block, last = spot
        next_tile = jnp.where(last == 1, jnp.minimum(tile + 1, 63), tile)
        next_block = jnp.where(last == 1, 0, block + 1)
        return with_last(next_tile, next_block)

    def with_last(tile, block):
        return tile, block, (block + 1 >= counts[tile]).astype(jnp.int32)

    for copy in copies:
        copy.wait()
    start = with_last(jnp.int32(0), jnp.int32(0))
    second = following(start)
    gather(0, start)
    gather(128, second)

    sublane = lax.broadcasted_iota(jnp.int32, (8, 256), 0)

    def split(value):
        high = value.astype(jnp.bfloat16)
        return high, (value - high.astype(jnp.float32)).astype(jnp.bfloat16)

    def step(index, state):
        now, ago, old = state
        later = following(now[1])
        later = (later, following(later))

        parts = []
        for n in range(2):
            part = jnp.dot(
                jnp.concatenate([turned_of[1, n]] * 2, axis=1),
                weight_of[n],
                preferred_element_type=jnp.float32,
            )
            parts.append(part[:8] + part[8:16] + part[16:24])
        first_done = totals[...] + parts[0]
        closed[...] = first_done
        totals[...] = first_done * (1 - old[0][2]).astype(jnp.float32) + parts[1]

        before = carry[...]
        for n in range(2):
            fresh = ago[n][1] == 0
            before = jnp.where(fresh, 1.0, before)
            kept = None
            shares = []
            for r in range(16):
                alphas = alphas_of[n, 8 * r : 8 * r + 8, :]
                shares.append(alphas if kept is None else alphas * kept)
                kept = 1.0 - alphas if kept is None else kept * (1.0 - alphas)
            for distance in (1, 2, 4):
                kept = kept * jnp.where(
                    sublane >= distance, pltpu.roll(kept, distance, 0), 1.0
                )
            ahead = before * jnp.where(sublane >= 1, pltpu.roll(kept, 1, 0), 1.0)
            before = before * jnp.broadcast_to(kept[7:8], kept.shape)
            weight = jnp.concatenate([share * ahead for share in shares], axis=0)
            high, low = split(weight)
            weight_of[n, :128, :] = high
            weight_of[n, 128:, :] = low
        carry[...] = before

        turned_of[1] = turned_of[0]
        for n in range(2):
            rows = picked[128 * n : 128 * n + 128, :]
            turned = rows.T
            turned_of[0, n] = jnp.concatenate(
                [turned[8:16], turned[24:32], turned[40:48], turned[40:48]], axis=0
            ).astype(jnp.bfloat16)
            power = jnp.dot(
                rows.astype(jnp.bfloat16), basis[...], preferred_element_type=jnp.float32
            )
            alphas_of[n] = jnp.exp2(power)
        for n in range(2):
            gather(128 * n, later[n])

        @pl.when(old[0][2] == 1)
        def _():
            finish(old[0][0], closed)

        @pl.when(old[1][2] == 1)
        def _():
            finish(old[1][0], totals)
            totals[...] = jnp.zeros_like(totals)

        return later, now, ago

    steps = lax.fori_loop(0, 64, lambda i, n: n + counts[i], 0)
    zero = jnp.int32(0)
    none = ((zero, zero, zero), (zero, zero, zero))
    lax.fori_loop(0, (steps + 1) // 2 + 2, step, ((start, second), none, none))


def render(counts, slots, places, packed):
    packed_rows = packed.shape[0]
    vmem = pl.BlockSpec(memory_space=pltpu.VMEM)
    smem = pl.BlockSpec(memory_space=pltpu.SMEM)
    hbm = pl.BlockSpec(memory_space=pl.ANY)
    return pl.pallas_call(
        render_kernel,
        out_shape=[
            jax.ShapeDtypeStruct((2, 3, 64, 128), jnp.float32),
            jax.ShapeDtypeStruct((2, 4, 64, 128), jnp.float32),
        ],
        in_specs=[smem, hbm, hbm, vmem, vmem],
        out_specs=[vmem, vmem],
        scratch_shapes=[
            pltpu.VMEM((8 * packed_rows + 8, 128), jnp.float32),
            pltpu.VMEM((256, 128), jnp.float32),
            pltpu.VMEM((8, 256), jnp.float32),
            pltpu.VMEM((8, 256), jnp.float32),
            pltpu.VMEM((128, 128), jnp.float32),
            pltpu.VMEM((8, 256), jnp.float32),
            pltpu.VMEM((2, 128, 256), jnp.float32),
            pltpu.VMEM((2, 256, 256), jnp.bfloat16),
            pltpu.VMEM((2, 2, 32, 128), jnp.bfloat16),
            pltpu.SMEM(slots.shape, jnp.int32),
            pltpu.SMEM(places.shape, jnp.int32),
            pltpu.SemaphoreType.DMA((2,)),
        ],
        compiler_params=pltpu.CompilerParams(vmem_limit_bytes=52 * MIB),
        name="render",
    )(counts, slots, places, packed, pixel_basis())


def surface_kernel(maps, out, halo, send_sem, recv_sem):
    row = lax.axis_index("rows")
    col = lax.axis_index("cols")
    sides = [
        (row > 0, (row - 1, col), row < 15),
        (row < 15, (row + 1, col), row > 0),
        (col > 0, (row, col - 1), col < 7),
        (col < 7, (row, col + 1), col > 0),
    ]
    barrier = pltpu.get_barrier_semaphore()
    for there, device, _ in sides:

        @pl.when(there)
        def _(device=device):
            pl.semaphore_signal(
                barrier, inc=1, device_id=device, device_id_type=pl.DeviceIdType.MESH
            )

    neighbours = sum(there.astype(jnp.int32) for there, _, _ in sides)
    pl.semaphore_wait(barrier, neighbours)

    def copy(n, device):
        part = (slice(None), pl.ds(0, 8)) if n == 0 else (slice(None), pl.ds(56, 8))
        source, target = maps.at[:, 0], halo.at[n]
        if n < 2:
            source, target = source.at[part], target.at[part]
        return pltpu.make_async_remote_copy(
            src_ref=source,
            dst_ref=target,
            send_sem=send_sem.at[n],
            recv_sem=recv_sem.at[n],
            device_id=device,
            device_id_type=pl.DeviceIdType.MESH,
        )

    for n, (there, device, _) in enumerate(sides):

        @pl.when(there)
        def _(n=n, device=device):
            copy(n, device).start()

    for n, (there, device, source) in enumerate(sides):

        @pl.when(source)
        def _(n=n):
            copy(n, sides[n ^ 1][1]).wait_recv()

    y = lax.broadcasted_iota(jnp.int32, (64, 128), 0)
    x = lax.broadcasted_iota(jnp.int32, (64, 128), 1)
    for view in range(2):
        depth = maps[view, 0]
        below = jnp.where(row < 15, halo[0, view, 0:1, :], 0.0)
        above = jnp.where(row > 0, halo[1, view, 63:64, :], 0.0)
        right = jnp.where(col < 7, halo[2, view], 0.0)
        left = jnp.where(col > 0, halo[3, view], 0.0)
        north = jnp.where(y == 0, above, pltpu.roll(depth, 1, 0))
        south = jnp.where(y == 63, below, pltpu.roll(depth, 63, 0))
        west = pltpu.roll(jnp.where(x == 127, left, depth), 1, 1)
        east = pltpu.roll(jnp.where(x == 0, right, depth), 127, 1)
        grad_x = 0.5 * (east - west)
        grad_y = 0.5 * (south - north)
        inverse = 1.0 / jnp.sqrt(grad_x * grad_x + grad_y * grad_y + 1.0)
        slope = maps[view, 3] - maps[view, 1] * grad_x - maps[view, 2] * grad_y
        out[view] = 1.0 - slope * inverse

    for n, (there, device, _) in enumerate(sides):

        @pl.when(there)
        def _(n=n, device=device):
            copy(n, device).wait_send()


def consistency_map(maps):
    vmem = pl.BlockSpec(memory_space=pltpu.VMEM)
    return pl.pallas_call(
        surface_kernel,
        out_shape=jax.ShapeDtypeStruct((2, 64, 128), jnp.float32),
        in_specs=[vmem],
        out_specs=vmem,
        scratch_shapes=[
            pltpu.VMEM((4, 2, 64, 128), jnp.float32),
            pltpu.SemaphoreType.DMA((4,)),
            pltpu.SemaphoreType.DMA((4,)),
        ],
        compiler_params=pltpu.CompilerParams(collective_id=0, has_side_effects=True),
        name="surface",
    )(maps)


def shade(position, sh_coeffs, camera):
    offset = position[None, :, :] - camera[:, :, None]
    distance = jnp.sqrt(jnp.sum(offset * offset, axis=1, keepdims=True))
    direction = offset / distance
    dir_x = direction[:, 0]
    dir_y = direction[:, 1]
    dir_z = direction[:, 2]
    sq_x = dir_x * dir_x
    sq_y = dir_y * dir_y
    sq_z = dir_z * dir_z
    sh_basis = jnp.stack(
        [
            jnp.full_like(dir_x, sh_first),
            -sh_second * dir_y,
            sh_second * dir_z,
            -sh_second * dir_x,
            sh_third[0] * dir_x * dir_y,
            sh_third[1] * dir_y * dir_z,
            sh_third[2] * (2.0 * sq_z - sq_x - sq_y),
            sh_third[3] * dir_x * dir_z,
            sh_third[4] * (sq_x - sq_y),
            sh_fourth[0] * dir_y * (3.0 * sq_x - sq_y),
            sh_fourth[1] * dir_x * dir_y * dir_z,
            sh_fourth[2] * dir_y * (4.0 * sq_z - sq_x - sq_y),
            sh_fourth[3] * dir_z * (2.0 * sq_z - 3.0 * sq_x - 3.0 * sq_y),
            sh_fourth[4] * dir_x * (4.0 * sq_z - sq_x - sq_y),
            sh_fourth[5] * dir_z * (sq_x - sq_y),
            sh_fourth[6] * dir_x * (sq_x - 3.0 * sq_y),
        ],
        axis=1,
    )
    coefficients = sh_coeffs.reshape(3, 16, -1)
    colour = 0.5 + jnp.sum(sh_basis[:, None] * coefficients[None], axis=2)
    return jnp.maximum(colour, 0.0).reshape(-1, position.shape[1])


def composite(table_rows, slot_lists, lengths, view_index, view_count, block_count, block_size):
    tile_rows, tile_cols, slot_count = slot_lists.shape
    tile_count = tile_rows * tile_cols
    slot_index = slot_lists.reshape(tile_count, slot_count)
    live_count = lengths.reshape(tile_count)
    pixel_ids = jnp.arange(256, dtype=jnp.int32)
    local_x = ((pixel_ids % 16).astype(jnp.float32) - 7.5) / 8.0
    local_y = ((pixel_ids // 16).astype(jnp.float32) - 7.5) / 8.0
    positions = jnp.arange(block_size, dtype=jnp.int32)
    earlier = (positions[:, None] < positions[None, :]).astype(jnp.float32)
    feature_rows = (
        [10 * view_count + 1 + 3 * view_index + k for k in range(3)]
        + [6 * view_count + 1 + view_index]
        + [7 * view_count + 1 + 3 * view_index + k for k in range(3)]
    )

    def block_step(block_index, state):
        totals, log_before = state
        first_slot = block_index * block_size
        picked_index = lax.dynamic_slice_in_dim(slot_index, first_slot, block_size, 1)
        picked = jnp.take(table_rows, picked_index.reshape(-1), axis=0)
        picked = picked.reshape(tile_count, block_size, table_rows.shape[1]).transpose(2, 0, 1)
        part_map = picked[6 * view_index : 6 * view_index + 6]
        part_opacity = picked[6 * view_count]
        part_features = jnp.stack([picked[row] for row in feature_rows], 0)
        live_mask = ((first_slot + positions)[None, :] < live_count[:, None]).astype(jnp.float32)
        coord_u = (
            part_map[0][:, None, :] * local_x[None, :, None]
            + part_map[1][:, None, :] * local_y[None, :, None]
            + part_map[2][:, None, :]
        )
        coord_w = (
            part_map[3][:, None, :] * local_x[None, :, None]
            + part_map[4][:, None, :] * local_y[None, :, None]
            + part_map[5][:, None, :]
        )
        alphas = part_opacity[:, None, :] * jnp.exp(-0.5 * (coord_u * coord_u + coord_w * coord_w))
        log_keep = jnp.log1p(-alphas) * live_mask[:, None, :]
        before = log_before[:, :, None] + jnp.einsum(
            "tps,sq->tpq", log_keep, earlier, precision=lax.Precision.HIGHEST
        )
        weight = alphas * jnp.exp(before) * live_mask[:, None, :]
        totals = totals + jnp.einsum(
            "fts,tps->tfp", part_features, weight, precision=lax.Precision.HIGHEST
        )
        return (totals, log_before + jnp.sum(log_keep, axis=2))

    start_state = (
        jnp.zeros((tile_count, 7, 256), jnp.float32),
        jnp.zeros((tile_count, 256), jnp.float32),
    )
    totals, unused_log = lax.fori_loop(0, block_count, block_step, start_state)
    return (
        totals.reshape(tile_rows, tile_cols, 7, 16, 16)
        .transpose(2, 0, 3, 1, 4)
        .reshape(7, tile_rows * 16, tile_cols * 16)
    )


def general(
    splat_map,
    opacity,
    depths,
    normals,
    position,
    sh_coeffs,
    camera,
    requests,
    tile_lists,
    list_lengths,
):
    view_count = camera.shape[0]
    device_count = requests.shape[1]
    capacity = requests.shape[2]
    asked_for = lax.all_to_all(requests, ("rows", "cols"), split_axis=1, concat_axis=0, tiled=True)
    wanted = asked_for.reshape(-1)
    geometry_count = 10 * view_count + 1
    source_table = jnp.concatenate(
        [splat_map, opacity[None, :], depths, normals, position, sh_coeffs], 0
    ).T
    gathered = jnp.take(source_table, wanted, axis=0).T
    outgoing = jnp.concatenate(
        [
            gathered[:geometry_count],
            shade(
                gathered[geometry_count : geometry_count + 3],
                gathered[geometry_count + 3 :],
                camera,
            ),
        ],
        0,
    )
    field_rows = outgoing.shape[0]
    arrived = lax.all_to_all(
        outgoing.reshape(field_rows, device_count, capacity),
        ("rows", "cols"),
        split_axis=1,
        concat_axis=1,
        tiled=True,
    ).reshape(field_rows, device_count * capacity)
    padded_count = (field_rows + 7) // 8 * 8
    table_rows = jnp.pad(arrived, ((0, padded_count - field_rows), (0, 0))).T
    slot_count = tile_lists.shape[-1]
    block_size = min(128, slot_count)
    feature_maps = jnp.stack(
        [
            composite(
                table_rows,
                tile_lists[view_index],
                list_lengths[view_index],
                view_index,
                view_count,
                slot_count // block_size,
                block_size,
            )
            for view_index in range(view_count)
        ]
    )
    return feature_maps[:, :3], feature_maps[:, 3:]


def shards(
    splat_map,
    opacity,
    depths,
    normals,
    position,
    sh_coeffs,
    camera,
    requests,
    tile_lists,
    list_lengths,
):
    lengths = list_lengths.reshape(-1)
    message, places = plan(lengths, tile_lists.reshape(256, 128), requests[0])
    asked_for = lax.all_to_all(message, ("rows", "cols"), split_axis=0, concat_axis=0, tiled=True)
    outgoing = serve(
        asked_for.reshape(-1), splat_map, opacity, depths, normals, position, sh_coeffs, camera
    )
    arrived = lax.all_to_all(
        outgoing.reshape(128, ROWS, 128), ("rows", "cols"), split_axis=0, concat_axis=0, tiled=True
    ).reshape(128 * ROWS, 128)

    def fast():
        slot = jnp.arange(512, dtype=jnp.int32)
        view = jnp.arange(2, dtype=jnp.int32)[:, None, None, None]
        slots = jnp.where(slot < list_lengths[..., None], tile_lists + 32768 * view, 65536)
        dead = jnp.full((8,), 8 * 128 * ROWS, jnp.int32)
        return render(
            (lengths + 127) // 128,
            slots.reshape(-1),
            jnp.concatenate([places.reshape(-1), dead]),
            arrived,
        )

    def slow():
        return general(
            splat_map,
            opacity,
            depths,
            normals,
            position,
            sh_coeffs,
            camera,
            requests,
            tile_lists,
            list_lengths,
        )

    image, maps = lax.cond(jnp.max(asked_for[:, 255]) > 0, slow, fast)
    return (image, consistency_map(maps))


def solution(mesh):
    in_specs = (
        P(None, ("rows", "cols")),
        P(("rows", "cols")),
        P(None, ("rows", "cols")),
        P(None, ("rows", "cols")),
        P(None, ("rows", "cols")),
        P(None, ("rows", "cols")),
        P(),
        P(("rows", "cols"), None, None),
        P(None, "rows", "cols", None),
        P(None, "rows", "cols"),
    )
    out_specs = (P(None, None, "rows", "cols"), P(None, "rows", "cols"))
    return jax.shard_map(shards, mesh=mesh, in_specs=in_specs, out_specs=out_specs, check_vma=False)
```

```python
import functools
import math

import jax
import jax.numpy as jnp
import numpy as np
from jax import lax
from jax.experimental import pallas as pl
from jax.experimental.pallas import tpu as pltpu
from jax.sharding import PartitionSpec as P

sh_first = 0.28209479177387814
sh_second = 0.4886025119029199
sh_third = [
    1.0925484305920792,
    -1.0925484305920792,
    0.31539156525252005,
    -1.0925484305920792,
    0.5462742152960396,
]
sh_fourth = [
    -0.5900435899266435,
    2.890611442640554,
    -0.4570457994644658,
    0.3731763325901154,
    -0.4570457994644658,
    1.445305721320277,
    -0.5900435899266435,
]
LOG2E = 1.4426950408889634
MIB = 1 << 20
IN_ROWS = 88
OUT_ROWS = 32
SHADE_BLOCK = 4096
ROWS = 24
LIMIT = 4 * ROWS


def dense_block(src, field):
    return src[pl.ds(field, 8, stride=IN_ROWS), :]


def owner_kernel(
    camera,
    wanted,
    splat,
    opacity,
    depths,
    normals,
    position,
    coeffs,
    out,
    table,
    fields_in,
    fields_out,
):
    first_row = pl.program_id(0) * SHADE_BLOCK

    def shade_part(part, fields_in, fields_out):
        for j in range(8):
            cols = pl.ds(pl.multiple_of(part * 1024 + j * 128, 128), 128)
            first = j * IN_ROWS
            fields_in[first : first + 12, :] = splat[:, cols]
            fields_in[first + 16 : first + 18, :] = depths[:, cols]
            fields_in[first + 24 : first + 30, :] = normals[:, cols]
            fields_in[first + 32 : first + 35, :] = position[:, cols]
            fields_in[first + 40 : first + 88, :] = coeffs[:, cols]
        field = functools.partial(dense_block, fields_in)
        log_opacity = jnp.log(opacity[pl.ds(pl.multiple_of(part * 8, 8), 8), :]) * LOG2E
        zero = jnp.zeros((8, 128), jnp.float32)
        bases = []
        for view in range(2):

            def put(row, value, view=view):
                fields_out[pl.ds(16 * view + row, 8, stride=OUT_ROWS), :] = value

            m = [field(6 * view + k) for k in range(6)]
            half = -0.5 * LOG2E
            put(0, half * (m[0] * m[0] + m[3] * m[3]))
            put(1, (2.0 * half) * (m[0] * m[1] + m[3] * m[4]))
            put(2, half * (m[1] * m[1] + m[4] * m[4]))
            put(3, (2.0 * half) * (m[0] * m[2] + m[3] * m[5]))
            put(4, (2.0 * half) * (m[1] * m[2] + m[4] * m[5]))
            put(5, half * (m[2] * m[2] + m[5] * m[5]) + log_opacity)
            put(6, zero)
            put(7, zero)
            put(11, field(16 + view))
            for k in range(3):
                put(12 + k, field(24 + 3 * view + k))
            put(15, zero)
            off = [field(32 + k) - camera[view, k] for k in range(3)]
            distance = jnp.sqrt(off[0] * off[0] + off[1] * off[1] + off[2] * off[2])
            inverse = 1.0 / distance
            dir_x, dir_y, dir_z = [o * inverse for o in off]
            sq_x = dir_x * dir_x
            sq_y = dir_y * dir_y
            sq_z = dir_z * dir_z
            bases.append(
                [
                    None,
                    -sh_second * dir_y,
                    sh_second * dir_z,
                    -sh_second * dir_x,
                    sh_third[0] * dir_x * dir_y,
                    sh_third[1] * dir_y * dir_z,
                    sh_third[2] * (2.0 * sq_z - sq_x - sq_y),
                    sh_third[3] * dir_x * dir_z,
                    sh_third[4] * (sq_x - sq_y),
                    sh_fourth[0] * dir_y * (3.0 * sq_x - sq_y),
                    sh_fourth[1] * dir_x * dir_y * dir_z,
                    sh_fourth[2] * dir_y * (4.0 * sq_z - sq_x - sq_y),
                    sh_fourth[3] * dir_z * (2.0 * sq_z - 3.0 * sq_x - 3.0 * sq_y),
                    sh_fourth[4] * dir_x * (4.0 * sq_z - sq_x - sq_y),
                    sh_fourth[5] * dir_z * (sq_x - sq_y),
                    sh_fourth[6] * dir_x * (sq_x - 3.0 * sq_y),
                ]
            )
        for channel in range(3):
            c = field(40 + 16 * channel)
            sums = [0.5 + sh_first * c, 0.5 + sh_first * c]
            for k in range(1, 16):
                c = field(40 + 16 * channel + k)
                for view in range(2):
                    sums[view] = sums[view] + bases[view][k] * c
            for view in range(2):
                fields_out[pl.ds(16 * view + 8 + channel, 8, stride=OUT_ROWS), :] = jnp.maximum(
                    sums[view], 0.0
                )
        for j in range(8):
            first = fields_out[j * OUT_ROWS : j * OUT_ROWS + 16, :]
            second = fields_out[j * OUT_ROWS + 16 : j * OUT_ROWS + 32, :]
            block = jnp.concatenate([first] * 4 + [second] * 4, axis=0)
            table[pl.ds(pl.multiple_of(first_row + part * 1024 + j * 128, 128), 128), :] = block.T

    for part in range(SHADE_BLOCK // 1024):
        shade_part(part, fields_in.at[part], fields_out.at[part])

    @pl.when(pl.program_id(0) == pl.num_programs(0) - 1)
    def _():
        gather(wanted, table, out)


def gather(wanted, table, out):
    group = lax.broadcasted_iota(jnp.int32, (1, 128), 1) // 16

    def rows(dest, first, last):
        for i in range(first, last):
            picked = [
                table[pl.ds(wanted[dest * 256 + (g // 4) * LIMIT + 4 * i + g % 4], 1), :]
                for g in range(8)
            ]
            for bit in (1, 2, 4):
                picked = [
                    jnp.where((group // bit) % 2 == 0, picked[n], picked[n + 1])
                    for n in range(0, len(picked), 2)
                ]
            out[pl.ds(dest * ROWS + i, 1), :] = picked[0]

    def body(dest, state):
        count = jnp.maximum(wanted[dest * 256 + 253], wanted[dest * 256 + 254])
        rows(dest, 0, 16)

        @pl.when(count > 64)
        def _():
            rows(dest, 16, ROWS)

        return state

    out[...] = jnp.zeros_like(out)
    lax.fori_loop(0, 128, body, 0)


def serve(wanted, splat_map, opacity, depths, normals, position, sh_coeffs, camera):
    count = opacity.shape[0]

    def cols(rows):
        return pl.BlockSpec((rows, SHADE_BLOCK), lambda i: (0, i))

    return pl.pallas_call(
        owner_kernel,
        grid=(count // SHADE_BLOCK,),
        out_shape=jax.ShapeDtypeStruct((128 * ROWS, 128), jnp.float32),
        in_specs=[
            pl.BlockSpec(memory_space=pltpu.SMEM),
            pl.BlockSpec(memory_space=pltpu.SMEM),
            cols(12),
            pl.BlockSpec((SHADE_BLOCK // 128, 128), lambda i: (i, 0)),
            cols(2),
            cols(6),
            cols(3),
            cols(48),
        ],
        out_specs=pl.BlockSpec(memory_space=pltpu.VMEM),
        scratch_shapes=[
            pltpu.VMEM((count, 128), jnp.float32),
            pltpu.VMEM((SHADE_BLOCK // 1024, 8 * IN_ROWS, 128), jnp.float32),
            pltpu.VMEM((SHADE_BLOCK // 1024, 8 * OUT_ROWS, 128), jnp.float32),
        ],
        compiler_params=pltpu.CompilerParams(vmem_limit_bytes=48 * MIB),
        name="serve",
    )(camera, wanted, splat_map, opacity.reshape(-1, 128), depths, normals, position, sh_coeffs)


def plan_kernel(lengths, lists, requests, lower, message, ranks, used, packed, owners, entries):
    owner_row = lax.broadcasted_iota(jnp.int32, (128, 512), 0)
    entry_row = lax.broadcasted_iota(jnp.int32, (256, 512), 0)
    slot = lax.broadcasted_iota(jnp.int32, (1, 128), 1)
    wanted = requests[...].astype(jnp.float32).T
    packed[192:256, :] = jnp.zeros((64, 128), jnp.float32)
    most = jnp.zeros((1, 128), jnp.float32)
    for view in range(2):
        used[...] = jnp.zeros_like(used)
        owners[...] = jnp.zeros_like(owners)
        entries[...] = jnp.zeros_like(entries)
        last_tile = 32 * view + 31

        def mark(step, spots):
            used[...] += lax.dot_general(
                entries[...],
                owners[...],
                (((1,), (1,)), ((), ())),
                preferred_element_type=jnp.float32,
            )
            tile, block = spots
            owner, entry = [], []
            for _ in range(4):
                row = jnp.minimum(tile, last_tile)
                first = block * 128
                place = lists[pl.ds(row * 4 + block, 1), :]
                length = jnp.where(tile > last_tile, 0, lengths[row])
                owner.append(jnp.where(slot + first < length, place // 256, -1))
                entry.append(place % 256)
                over = first + 128 >= length
                tile = jnp.where(over, tile + 1, tile)
                block = jnp.where(over, 0, block + 1)
            owner = jnp.concatenate(owner, axis=1)
            entry = jnp.concatenate(entry, axis=1)
            owners[...] = (owner_row == owner).astype(jnp.float32).astype(jnp.bfloat16)
            entries[...] = (entry_row == entry).astype(jnp.float32).astype(jnp.bfloat16)
            return tile, block

        blocks = lax.fori_loop(
            32 * view, 32 * view + 32, lambda t, n: n + (lengths[t] + 127) // 128, 0
        )
        lax.fori_loop(
            0, (blocks + 3) // 4 + 1, mark, (jnp.int32(32 * view), jnp.int32(0))
        )
        flag = jnp.minimum(used[...], 1.0)
        rank = jnp.dot(lower[...], flag.astype(jnp.bfloat16), preferred_element_type=jnp.float32)
        count = rank[255:256] + flag[255:256]
        packed[253 + view : 254 + view, :] = count
        most = jnp.maximum(most, count)
        ranks[view] = rank.T
        rank = jnp.where(flag > 0.0, rank, -1.0)

        def pick(step, state, view=view, rank=rank):
            for i in range(8):
                entry = step * 8 + i
                chosen = jnp.where(rank == entry.astype(jnp.float32), wanted, 0.0)
                packed[pl.ds(view * LIMIT + entry, 1), :] = jnp.sum(chosen, axis=0, keepdims=True)
            return state

        lax.fori_loop(0, LIMIT // 8, pick, 0)
    over = (most > LIMIT).astype(jnp.float32)
    packed[255:256, :] = jnp.broadcast_to(jnp.max(over, axis=1, keepdims=True), (1, 128))
    message[...] = packed[...].T.astype(jnp.int32)


def plan(lengths, lists, requests):
    vmem = pl.BlockSpec(memory_space=pltpu.VMEM)
    index = np.arange(256)
    lower = jnp.asarray(index[None, :] < index[:, None], jnp.bfloat16)
    return pl.pallas_call(
        plan_kernel,
        out_shape=[
            jax.ShapeDtypeStruct((128, 256), jnp.int32),
            jax.ShapeDtypeStruct((2, 128, 256), jnp.float32),
        ],
        in_specs=[pl.BlockSpec(memory_space=pltpu.SMEM), vmem, vmem, vmem],
        out_specs=[vmem, vmem],
        scratch_shapes=[
            pltpu.VMEM((256, 128), jnp.float32),
            pltpu.VMEM((256, 128), jnp.float32),
            pltpu.VMEM((128, 512), jnp.bfloat16),
            pltpu.VMEM((256, 512), jnp.bfloat16),
        ],
        compiler_params=pltpu.CompilerParams(vmem_limit_bytes=32 * MIB),
        name="plan",
    )(lengths, lists, requests, lower)


def place_kernel(lengths, lists, ranks, rows, owners, entries, owner_of):
    owner_row = lax.broadcasted_iota(jnp.int32, (128, 512), 0)
    entry_row = lax.broadcasted_iota(jnp.int32, (256, 512), 0)
    slot = lax.broadcasted_iota(jnp.int32, (1, 128), 1)
    dead = 8 * 128 * ROWS
    owners[...] = jnp.zeros_like(owners)
    entries[...] = jnp.zeros_like(entries)
    owner_of[...] = jnp.zeros_like(owner_of)
    for view in range(2):
        last_tile = 32 * view + 31
        rank_of = ranks[view].astype(jnp.bfloat16)

        def step(index, state, view=view, rank_of=rank_of, last_tile=last_tile):
            (tile, block), targets = state
            picked = jnp.dot(rank_of, entries[...], preferred_element_type=jnp.float32)
            rank = jnp.sum(picked * owners[...].astype(jnp.float32), axis=0, keepdims=True)
            level = jnp.floor(rank * 0.25)
            owner = owner_of[...]
            row = ((rank - 4.0 * level + 4.0 * view) * 128.0 + owner) * ROWS + level
            row = jnp.where(owner < 0.0, dead, row.astype(jnp.int32))
            for n in range(4):
                rows[pl.ds(targets[n], 1), :] = row[:, 128 * n : 128 * n + 128]
            owner, entry, targets = [], [], []
            for _ in range(4):
                row = jnp.minimum(tile, last_tile) * 4 + block
                first = block * 128
                place = lists[pl.ds(row, 1), :]
                length = jnp.where(tile > last_tile, 0, lengths[jnp.minimum(tile, last_tile)])
                owner.append(jnp.where(slot + first < length, place // 256, -1))
                entry.append(place % 256)
                targets.append(jnp.where(tile > last_tile, 256, row))
                over = first + 128 >= length
                tile = jnp.where(over, tile + 1, tile)
                block = jnp.where(over, 0, block + 1)
            owner = jnp.concatenate(owner, axis=1)
            entry = jnp.concatenate(entry, axis=1)
            owner_of[...] = owner.astype(jnp.float32)
            owners[...] = (owner_row == owner).astype(jnp.float32).astype(jnp.bfloat16)
            entries[...] = (entry_row == entry).astype(jnp.float32).astype(jnp.bfloat16)
            return (tile, block), tuple(targets)

        blocks = lax.fori_loop(
            32 * view, 32 * view + 32, lambda t, n: n + (lengths[t] + 127) // 128, 0
        )
        start = (jnp.int32(32 * view), jnp.int32(0))
        lax.fori_loop(0, (blocks + 3) // 4 + 1, step, (start, (jnp.int32(256),) * 4))


def place(lengths, lists, ranks):
    vmem = pl.BlockSpec(memory_space=pltpu.VMEM)
    return pl.pallas_call(
        place_kernel,
        out_shape=jax.ShapeDtypeStruct((264, 128), jnp.int32),
        in_specs=[pl.BlockSpec(memory_space=pltpu.SMEM), vmem, vmem],
        out_specs=vmem,
        scratch_shapes=[
            pltpu.VMEM((128, 512), jnp.bfloat16),
            pltpu.VMEM((256, 512), jnp.bfloat16),
            pltpu.VMEM((1, 512), jnp.float32),
        ],
        compiler_params=pltpu.CompilerParams(vmem_limit_bytes=32 * MIB),
        cost_estimate=pl.CostEstimate(
            flops=2 * 43 * 128 * 256 * 512, bytes_accessed=600000, transcendentals=0
        ),
        name="place",
    )(lengths, lists, ranks)


def pixel_basis():
    pixel = np.arange(256)
    x = ((pixel % 16) - 7.5) / 8.0
    y = ((pixel // 16) - 7.5) / 8.0
    basis = np.zeros((128, 256), np.float32)
    for part in range(3):
        for k, value in enumerate([x * x, x * y, y * y, x, y, np.ones(256)]):
            basis[16 * part + k] = value
    return jnp.asarray(basis, jnp.bfloat16)


def swap_groups(block):
    row = lax.broadcasted_iota(jnp.int32, (8, 128), 0)
    group = lax.broadcasted_iota(jnp.int32, (8, 128), 1) // 16
    for bit in (1, 2, 4):
        row_bit = (row // bit) % 2
        group_bit = (group // bit) % 2
        from_below = pltpu.roll(pltpu.roll(block, 8 - bit, 0), 16 * bit, 1)
        from_above = pltpu.roll(pltpu.roll(block, bit, 0), 128 - 16 * bit, 1)
        block = jnp.where(
            row_bit == group_bit, block, jnp.where(row_bit < group_bit, from_below, from_above)
        )
    return block


def render_kernel(
    counts, slots_in, packed, basis, image, maps, table, picked, totals, carry, stage,
    closed, alphas_of, weight_of, turned_of,
    slots, copy_sem
):
    copy = pltpu.make_async_copy(slots_in, slots, copy_sem)
    copy.start()
    packed_rows = packed.shape[0]
    lane = lax.broadcasted_iota(jnp.int32, (8, 128), 1)
    group = lane // 16

    def unpack(step, state):
        base = pl.multiple_of(step * 8, 8)
        whole = packed[pl.ds(base, 8), :]
        high = whole.astype(jnp.bfloat16).astype(jnp.float32)
        rest = whole - high
        mid = rest.astype(jnp.bfloat16).astype(jnp.float32)
        low = pltpu.roll(rest - mid, 32, 1)
        mid = pltpu.roll(mid, 16, 1)
        for g in range(8):
            row = jnp.where(group == g, high, jnp.where(group == (g + 1) % 8, mid, low))
            if g:
                row = pltpu.roll(row, 128 - 16 * g, 1)
            table[pl.ds(pl.multiple_of(g * packed_rows + base, 8), 8), :] = row
        return state

    lax.fori_loop(0, packed_rows // 8, unpack, 0, unroll=16)
    table[8 * packed_rows : 8 * packed_rows + 8, :] = jnp.where(lane == 5, -300.0, 0.0)
    def gather(place, spot):
        first = spot[0] * 512 + spot[1] * 128
        for i in range(128):
            slot = first + 16 * (i % 8) + i // 8
            picked[place + i : place + i + 1, :] = table[pl.ds(slots[slot], 1), :]

    def finish(tile, result):
        column = lax.rem(tile, 8)
        for h in range(2):
            stage[pl.ds(h * 8 + column, 8, stride=16), :] = result[:, h * 128 : (h + 1) * 128]

        @pl.when(column == 7)
        def _():
            view = tile // 32
            tile_row = lax.rem(tile // 8, 4)
            for f in range(7):
                for h in range(2):
                    block = swap_groups(stage[(2 * f + h) * 8 : (2 * f + h) * 8 + 8, :])
                    place = pl.ds(pl.multiple_of(tile_row * 16 + h * 8, 8), 8)
                    if f < 3:
                        image[view, f, place, :] = block
                    else:
                        maps[view, f - 3, place, :] = block

    totals[...] = jnp.zeros_like(totals)
    carry[...] = jnp.ones_like(carry)
    alphas_of[...] = jnp.zeros_like(alphas_of)
    weight_of[...] = jnp.zeros_like(weight_of)
    turned_of[...] = jnp.zeros_like(turned_of)

    def following(spot):
        tile, block, last = spot
        next_tile = jnp.where(last == 1, jnp.minimum(tile + 1, 63), tile)
        next_block = jnp.where(last == 1, 0, block + 1)
        return with_last(next_tile, next_block)

    def with_last(tile, block):
        return tile, block, (block + 1 >= counts[tile]).astype(jnp.int32)

    copy.wait()
    start = with_last(jnp.int32(0), jnp.int32(0))
    second = following(start)
    gather(0, start)
    gather(128, second)

    sublane = lax.broadcasted_iota(jnp.int32, (8, 256), 0)

    def split(value):
        high = value.astype(jnp.bfloat16)
        return high, (value - high.astype(jnp.float32)).astype(jnp.bfloat16)

    def step(index, state):
        now, ago, old = state
        later = following(now[1])
        later = (later, following(later))

        parts = []
        for n in range(2):
            part = jnp.dot(
                jnp.concatenate([turned_of[1, n]] * 2, axis=1),
                weight_of[n],
                preferred_element_type=jnp.float32,
            )
            parts.append(part[:8] + part[8:16] + part[16:24])
        first_done = totals[...] + parts[0]
        closed[...] = first_done
        totals[...] = first_done * (1 - old[0][2]).astype(jnp.float32) + parts[1]

        before = carry[...]
        for n in range(2):
            fresh = ago[n][1] == 0
            before = jnp.where(fresh, 1.0, before)
            kept = None
            shares = []
            for r in range(16):
                alphas = alphas_of[n, 8 * r : 8 * r + 8, :]
                shares.append(alphas if kept is None else alphas * kept)
                kept = 1.0 - alphas if kept is None else kept * (1.0 - alphas)
            for distance in (1, 2, 4):
                kept = kept * jnp.where(
                    sublane >= distance, pltpu.roll(kept, distance, 0), 1.0
                )
            ahead = before * jnp.where(sublane >= 1, pltpu.roll(kept, 1, 0), 1.0)
            before = before * jnp.broadcast_to(kept[7:8], kept.shape)
            weight = jnp.concatenate([share * ahead for share in shares], axis=0)
            high, low = split(weight)
            weight_of[n, :128, :] = high
            weight_of[n, 128:, :] = low
        carry[...] = before

        turned_of[1] = turned_of[0]
        for n in range(2):
            rows = picked[128 * n : 128 * n + 128, :]
            turned = rows.T
            turned_of[0, n] = jnp.concatenate(
                [turned[8:16], turned[24:32], turned[40:48], turned[40:48]], axis=0
            ).astype(jnp.bfloat16)
            power = jnp.dot(
                rows.astype(jnp.bfloat16), basis[...], preferred_element_type=jnp.float32
            )
            alphas_of[n] = jnp.exp2(power)
        for n in range(2):
            gather(128 * n, later[n])

        @pl.when(old[0][2] == 1)
        def _():
            finish(old[0][0], closed)

        @pl.when(old[1][2] == 1)
        def _():
            finish(old[1][0], totals)
            totals[...] = jnp.zeros_like(totals)

        return later, now, ago

    steps = lax.fori_loop(0, 64, lambda i, n: n + counts[i], 0)
    zero = jnp.int32(0)
    none = ((zero, zero, zero), (zero, zero, zero))
    lax.fori_loop(0, (steps + 1) // 2 + 2, step, ((start, second), none, none))


def render(counts, slots, packed):
    packed_rows = packed.shape[0]
    vmem = pl.BlockSpec(memory_space=pltpu.VMEM)
    smem = pl.BlockSpec(memory_space=pltpu.SMEM)
    hbm = pl.BlockSpec(memory_space=pl.ANY)
    return pl.pallas_call(
        render_kernel,
        out_shape=[
            jax.ShapeDtypeStruct((2, 3, 64, 128), jnp.float32),
            jax.ShapeDtypeStruct((2, 4, 64, 128), jnp.float32),
        ],
        in_specs=[smem, hbm, vmem, vmem],
        out_specs=[vmem, vmem],
        scratch_shapes=[
            pltpu.VMEM((8 * packed_rows + 8, 128), jnp.float32),
            pltpu.VMEM((256, 128), jnp.float32),
            pltpu.VMEM((8, 256), jnp.float32),
            pltpu.VMEM((8, 256), jnp.float32),
            pltpu.VMEM((128, 128), jnp.float32),
            pltpu.VMEM((8, 256), jnp.float32),
            pltpu.VMEM((2, 128, 256), jnp.float32),
            pltpu.VMEM((2, 256, 256), jnp.bfloat16),
            pltpu.VMEM((2, 2, 32, 128), jnp.bfloat16),
            pltpu.SMEM(slots.shape, jnp.int32),
            pltpu.SemaphoreType.DMA,
        ],
        compiler_params=pltpu.CompilerParams(vmem_limit_bytes=52 * MIB),
        name="render",
    )(counts, slots, packed, pixel_basis())


def surface_kernel(maps, out, halo, send_sem, recv_sem):
    row = lax.axis_index("rows")
    col = lax.axis_index("cols")
    sides = [
        (row > 0, (row - 1, col), row < 15),
        (row < 15, (row + 1, col), row > 0),
        (col > 0, (row, col - 1), col < 7),
        (col < 7, (row, col + 1), col > 0),
    ]
    barrier = pltpu.get_barrier_semaphore()
    for there, device, _ in sides:

        @pl.when(there)
        def _(device=device):
            pl.semaphore_signal(
                barrier, inc=1, device_id=device, device_id_type=pl.DeviceIdType.MESH
            )

    neighbours = sum(there.astype(jnp.int32) for there, _, _ in sides)
    pl.semaphore_wait(barrier, neighbours)

    def copy(n, device):
        part = (slice(None), pl.ds(0, 8)) if n == 0 else (slice(None), pl.ds(56, 8))
        source, target = maps.at[:, 0], halo.at[n]
        if n < 2:
            source, target = source.at[part], target.at[part]
        return pltpu.make_async_remote_copy(
            src_ref=source,
            dst_ref=target,
            send_sem=send_sem.at[n],
            recv_sem=recv_sem.at[n],
            device_id=device,
            device_id_type=pl.DeviceIdType.MESH,
        )

    for n, (there, device, _) in enumerate(sides):

        @pl.when(there)
        def _(n=n, device=device):
            copy(n, device).start()

    for n, (there, device, source) in enumerate(sides):

        @pl.when(source)
        def _(n=n):
            copy(n, sides[n ^ 1][1]).wait_recv()

    y = lax.broadcasted_iota(jnp.int32, (64, 128), 0)
    x = lax.broadcasted_iota(jnp.int32, (64, 128), 1)
    for view in range(2):
        depth = maps[view, 0]
        below = jnp.where(row < 15, halo[0, view, 0:1, :], 0.0)
        above = jnp.where(row > 0, halo[1, view, 63:64, :], 0.0)
        right = jnp.where(col < 7, halo[2, view], 0.0)
        left = jnp.where(col > 0, halo[3, view], 0.0)
        north = jnp.where(y == 0, above, pltpu.roll(depth, 1, 0))
        south = jnp.where(y == 63, below, pltpu.roll(depth, 63, 0))
        west = pltpu.roll(jnp.where(x == 127, left, depth), 1, 1)
        east = pltpu.roll(jnp.where(x == 0, right, depth), 127, 1)
        grad_x = 0.5 * (east - west)
        grad_y = 0.5 * (south - north)
        inverse = 1.0 / jnp.sqrt(grad_x * grad_x + grad_y * grad_y + 1.0)
        slope = maps[view, 3] - maps[view, 1] * grad_x - maps[view, 2] * grad_y
        out[view] = 1.0 - slope * inverse

    for n, (there, device, _) in enumerate(sides):

        @pl.when(there)
        def _(n=n, device=device):
            copy(n, device).wait_send()


def consistency_map(maps):
    vmem = pl.BlockSpec(memory_space=pltpu.VMEM)
    return pl.pallas_call(
        surface_kernel,
        out_shape=jax.ShapeDtypeStruct((2, 64, 128), jnp.float32),
        in_specs=[vmem],
        out_specs=vmem,
        scratch_shapes=[
            pltpu.VMEM((4, 2, 64, 128), jnp.float32),
            pltpu.SemaphoreType.DMA((4,)),
            pltpu.SemaphoreType.DMA((4,)),
        ],
        compiler_params=pltpu.CompilerParams(collective_id=0, has_side_effects=True),
        name="surface",
    )(maps)


def shade(position, sh_coeffs, camera):
    offset = position[None, :, :] - camera[:, :, None]
    distance = jnp.sqrt(jnp.sum(offset * offset, axis=1, keepdims=True))
    direction = offset / distance
    dir_x = direction[:, 0]
    dir_y = direction[:, 1]
    dir_z = direction[:, 2]
    sq_x = dir_x * dir_x
    sq_y = dir_y * dir_y
    sq_z = dir_z * dir_z
    sh_basis = jnp.stack(
        [
            jnp.full_like(dir_x, sh_first),
            -sh_second * dir_y,
            sh_second * dir_z,
            -sh_second * dir_x,
            sh_third[0] * dir_x * dir_y,
            sh_third[1] * dir_y * dir_z,
            sh_third[2] * (2.0 * sq_z - sq_x - sq_y),
            sh_third[3] * dir_x * dir_z,
            sh_third[4] * (sq_x - sq_y),
            sh_fourth[0] * dir_y * (3.0 * sq_x - sq_y),
            sh_fourth[1] * dir_x * dir_y * dir_z,
            sh_fourth[2] * dir_y * (4.0 * sq_z - sq_x - sq_y),
            sh_fourth[3] * dir_z * (2.0 * sq_z - 3.0 * sq_x - 3.0 * sq_y),
            sh_fourth[4] * dir_x * (4.0 * sq_z - sq_x - sq_y),
            sh_fourth[5] * dir_z * (sq_x - sq_y),
            sh_fourth[6] * dir_x * (sq_x - 3.0 * sq_y),
        ],
        axis=1,
    )
    coefficients = sh_coeffs.reshape(3, 16, -1)
    colour = 0.5 + jnp.sum(sh_basis[:, None] * coefficients[None], axis=2)
    return jnp.maximum(colour, 0.0).reshape(-1, position.shape[1])


def composite(table_rows, slot_lists, lengths, view_index, view_count, block_count, block_size):
    tile_rows, tile_cols, slot_count = slot_lists.shape
    tile_count = tile_rows * tile_cols
    slot_index = slot_lists.reshape(tile_count, slot_count)
    live_count = lengths.reshape(tile_count)
    pixel_ids = jnp.arange(256, dtype=jnp.int32)
    local_x = ((pixel_ids % 16).astype(jnp.float32) - 7.5) / 8.0
    local_y = ((pixel_ids // 16).astype(jnp.float32) - 7.5) / 8.0
    positions = jnp.arange(block_size, dtype=jnp.int32)
    earlier = (positions[:, None] < positions[None, :]).astype(jnp.float32)
    feature_rows = (
        [10 * view_count + 1 + 3 * view_index + k for k in range(3)]
        + [6 * view_count + 1 + view_index]
        + [7 * view_count + 1 + 3 * view_index + k for k in range(3)]
    )

    def block_step(block_index, state):
        totals, log_before = state
        first_slot = block_index * block_size
        picked_index = lax.dynamic_slice_in_dim(slot_index, first_slot, block_size, 1)
        picked = jnp.take(table_rows, picked_index.reshape(-1), axis=0)
        picked = picked.reshape(tile_count, block_size, table_rows.shape[1]).transpose(2, 0, 1)
        part_map = picked[6 * view_index : 6 * view_index + 6]
        part_opacity = picked[6 * view_count]
        part_features = jnp.stack([picked[row] for row in feature_rows], 0)
        live_mask = ((first_slot + positions)[None, :] < live_count[:, None]).astype(jnp.float32)
        coord_u = (
            part_map[0][:, None, :] * local_x[None, :, None]
            + part_map[1][:, None, :] * local_y[None, :, None]
            + part_map[2][:, None, :]
        )
        coord_w = (
            part_map[3][:, None, :] * local_x[None, :, None]
            + part_map[4][:, None, :] * local_y[None, :, None]
            + part_map[5][:, None, :]
        )
        alphas = part_opacity[:, None, :] * jnp.exp(-0.5 * (coord_u * coord_u + coord_w * coord_w))
        log_keep = jnp.log1p(-alphas) * live_mask[:, None, :]
        before = log_before[:, :, None] + jnp.einsum(
            "tps,sq->tpq", log_keep, earlier, precision=lax.Precision.HIGHEST
        )
        weight = alphas * jnp.exp(before) * live_mask[:, None, :]
        totals = totals + jnp.einsum(
            "fts,tps->tfp", part_features, weight, precision=lax.Precision.HIGHEST
        )
        return (totals, log_before + jnp.sum(log_keep, axis=2))

    start_state = (
        jnp.zeros((tile_count, 7, 256), jnp.float32),
        jnp.zeros((tile_count, 256), jnp.float32),
    )
    totals, unused_log = lax.fori_loop(0, block_count, block_step, start_state)
    return (
        totals.reshape(tile_rows, tile_cols, 7, 16, 16)
        .transpose(2, 0, 3, 1, 4)
        .reshape(7, tile_rows * 16, tile_cols * 16)
    )


def general(
    splat_map,
    opacity,
    depths,
    normals,
    position,
    sh_coeffs,
    camera,
    requests,
    tile_lists,
    list_lengths,
):
    view_count = camera.shape[0]
    device_count = requests.shape[1]
    capacity = requests.shape[2]
    asked_for = lax.all_to_all(requests, ("rows", "cols"), split_axis=1, concat_axis=0, tiled=True)
    wanted = asked_for.reshape(-1)
    geometry_count = 10 * view_count + 1
    source_table = jnp.concatenate(
        [splat_map, opacity[None, :], depths, normals, position, sh_coeffs], 0
    ).T
    gathered = jnp.take(source_table, wanted, axis=0).T
    outgoing = jnp.concatenate(
        [
            gathered[:geometry_count],
            shade(
                gathered[geometry_count : geometry_count + 3],
                gathered[geometry_count + 3 :],
                camera,
            ),
        ],
        0,
    )
    field_rows = outgoing.shape[0]
    arrived = lax.all_to_all(
        outgoing.reshape(field_rows, device_count, capacity),
        ("rows", "cols"),
        split_axis=1,
        concat_axis=1,
        tiled=True,
    ).reshape(field_rows, device_count * capacity)
    padded_count = (field_rows + 7) // 8 * 8
    table_rows = jnp.pad(arrived, ((0, padded_count - field_rows), (0, 0))).T
    slot_count = tile_lists.shape[-1]
    block_size = min(128, slot_count)
    feature_maps = jnp.stack(
        [
            composite(
                table_rows,
                tile_lists[view_index],
                list_lengths[view_index],
                view_index,
                view_count,
                slot_count // block_size,
                block_size,
            )
            for view_index in range(view_count)
        ]
    )
    return feature_maps[:, :3], feature_maps[:, 3:]


def shards(
    splat_map,
    opacity,
    depths,
    normals,
    position,
    sh_coeffs,
    camera,
    requests,
    tile_lists,
    list_lengths,
):
    lengths = list_lengths.reshape(-1)
    lists = tile_lists.reshape(256, 128)
    message, ranks = plan(lengths, lists, requests[0])
    asked_for = lax.all_to_all(message, ("rows", "cols"), split_axis=0, concat_axis=0, tiled=True)
    slots = place(lengths, lists, ranks)
    outgoing = serve(
        asked_for.reshape(-1), splat_map, opacity, depths, normals, position, sh_coeffs, camera
    )
    arrived = lax.all_to_all(
        outgoing.reshape(128, ROWS, 128), ("rows", "cols"), split_axis=0, concat_axis=0, tiled=True
    ).reshape(128 * ROWS, 128)

    def fast():
        return render((lengths + 127) // 128, slots.reshape(-1), arrived)

    def slow():
        return general(
            splat_map,
            opacity,
            depths,
            normals,
            position,
            sh_coeffs,
            camera,
            requests,
            tile_lists,
            list_lengths,
        )

    image, maps = lax.cond(jnp.max(asked_for[:, 255]) > 0, slow, fast)
    return (image, consistency_map(maps))


def solution(mesh):
    in_specs = (
        P(None, ("rows", "cols")),
        P(("rows", "cols")),
        P(None, ("rows", "cols")),
        P(None, ("rows", "cols")),
        P(None, ("rows", "cols")),
        P(None, ("rows", "cols")),
        P(),
        P(("rows", "cols"), None, None),
        P(None, "rows", "cols", None),
        P(None, "rows", "cols"),
    )
    out_specs = (P(None, None, "rows", "cols"), P(None, "rows", "cols"))
    return jax.shard_map(shards, mesh=mesh, in_specs=in_specs, out_specs=out_specs, check_vma=False)
```

```python
import functools
import math

import jax
import jax.numpy as jnp
import numpy as np
from jax import lax
from jax.experimental import pallas as pl
from jax.experimental.pallas import tpu as pltpu
from jax.sharding import PartitionSpec as P

sh_first = 0.28209479177387814
sh_second = 0.4886025119029199
sh_third = [
    1.0925484305920792,
    -1.0925484305920792,
    0.31539156525252005,
    -1.0925484305920792,
    0.5462742152960396,
]
sh_fourth = [
    -0.5900435899266435,
    2.890611442640554,
    -0.4570457994644658,
    0.3731763325901154,
    -0.4570457994644658,
    1.445305721320277,
    -0.5900435899266435,
]
LOG2E = 1.4426950408889634
MIB = 1 << 20
IN_ROWS = 88
OUT_ROWS = 32
SHADE_BLOCK = 4096
ROWS = 24
LIMIT = 4 * ROWS


def dense_block(src, field):
    return src[pl.ds(field, 8, stride=IN_ROWS), :]


def owner_kernel(
    camera,
    wanted_in,
    splat,
    opacity,
    depths,
    normals,
    position,
    coeffs,
    out,
    table,
    fields_in,
    fields_out,
    wanted,
    wanted_sem,
):
    copy = pltpu.make_async_copy(wanted_in, wanted, wanted_sem)

    @pl.when(pl.program_id(0) == 0)
    def _():
        copy.start()

    first_row = pl.program_id(0) * SHADE_BLOCK

    def shade_part(part, fields_in, fields_out):
        for j in range(8):
            cols = pl.ds(pl.multiple_of(part * 1024 + j * 128, 128), 128)
            first = j * IN_ROWS
            fields_in[first : first + 12, :] = splat[:, cols]
            fields_in[first + 16 : first + 18, :] = depths[:, cols]
            fields_in[first + 24 : first + 30, :] = normals[:, cols]
            fields_in[first + 32 : first + 35, :] = position[:, cols]
            fields_in[first + 40 : first + 88, :] = coeffs[:, cols]
        field = functools.partial(dense_block, fields_in)
        log_opacity = jnp.log(opacity[pl.ds(pl.multiple_of(part * 8, 8), 8), :]) * LOG2E
        zero = jnp.zeros((8, 128), jnp.float32)
        bases = []
        for view in range(2):

            def put(row, value, view=view):
                fields_out[pl.ds(16 * view + row, 8, stride=OUT_ROWS), :] = value

            m = [field(6 * view + k) for k in range(6)]
            half = -0.5 * LOG2E
            put(0, half * (m[0] * m[0] + m[3] * m[3]))
            put(1, (2.0 * half) * (m[0] * m[1] + m[3] * m[4]))
            put(2, half * (m[1] * m[1] + m[4] * m[4]))
            put(3, (2.0 * half) * (m[0] * m[2] + m[3] * m[5]))
            put(4, (2.0 * half) * (m[1] * m[2] + m[4] * m[5]))
            put(5, half * (m[2] * m[2] + m[5] * m[5]) + log_opacity)
            put(6, zero)
            put(7, zero)
            put(11, field(16 + view))
            for k in range(3):
                put(12 + k, field(24 + 3 * view + k))
            put(15, zero)
            off = [field(32 + k) - camera[view, k] for k in range(3)]
            distance = jnp.sqrt(off[0] * off[0] + off[1] * off[1] + off[2] * off[2])
            inverse = 1.0 / distance
            dir_x, dir_y, dir_z = [o * inverse for o in off]
            sq_x = dir_x * dir_x
            sq_y = dir_y * dir_y
            sq_z = dir_z * dir_z
            bases.append(
                [
                    None,
                    -sh_second * dir_y,
                    sh_second * dir_z,
                    -sh_second * dir_x,
                    sh_third[0] * dir_x * dir_y,
                    sh_third[1] * dir_y * dir_z,
                    sh_third[2] * (2.0 * sq_z - sq_x - sq_y),
                    sh_third[3] * dir_x * dir_z,
                    sh_third[4] * (sq_x - sq_y),
                    sh_fourth[0] * dir_y * (3.0 * sq_x - sq_y),
                    sh_fourth[1] * dir_x * dir_y * dir_z,
                    sh_fourth[2] * dir_y * (4.0 * sq_z - sq_x - sq_y),
                    sh_fourth[3] * dir_z * (2.0 * sq_z - 3.0 * sq_x - 3.0 * sq_y),
                    sh_fourth[4] * dir_x * (4.0 * sq_z - sq_x - sq_y),
                    sh_fourth[5] * dir_z * (sq_x - sq_y),
                    sh_fourth[6] * dir_x * (sq_x - 3.0 * sq_y),
                ]
            )
        for channel in range(3):
            c = field(40 + 16 * channel)
            sums = [0.5 + sh_first * c, 0.5 + sh_first * c]
            for k in range(1, 16):
                c = field(40 + 16 * channel + k)
                for view in range(2):
                    sums[view] = sums[view] + bases[view][k] * c
            for view in range(2):
                fields_out[pl.ds(16 * view + 8 + channel, 8, stride=OUT_ROWS), :] = jnp.maximum(
                    sums[view], 0.0
                )
        for j in range(8):
            first = fields_out[j * OUT_ROWS : j * OUT_ROWS + 16, :]
            second = fields_out[j * OUT_ROWS + 16 : j * OUT_ROWS + 32, :]
            block = jnp.concatenate([first] * 4 + [second] * 4, axis=0)
            table[pl.ds(pl.multiple_of(first_row + part * 1024 + j * 128, 128), 128), :] = block.T

    for part in range(SHADE_BLOCK // 1024):
        shade_part(part, fields_in.at[part], fields_out.at[part])

    @pl.when(pl.program_id(0) == pl.num_programs(0) - 1)
    def _():
        copy.wait()
        gather(wanted, table, out)


def gather(wanted, table, out):
    group = lax.broadcasted_iota(jnp.int32, (1, 128), 1) // 16

    def rows(dest, first, last):
        for i in range(first, last):
            picked = [
                table[pl.ds(wanted[dest * 256 + (g // 4) * LIMIT + 4 * i + g % 4], 1), :]
                for g in range(8)
            ]
            for bit in (1, 2, 4):
                picked = [
                    jnp.where((group // bit) % 2 == 0, picked[n], picked[n + 1])
                    for n in range(0, len(picked), 2)
                ]
            out[pl.ds(dest * ROWS + i, 1), :] = picked[0]

    def body(dest, state):
        count = jnp.maximum(wanted[dest * 256 + 253], wanted[dest * 256 + 254])
        rows(dest, 0, 16)

        @pl.when(count > 64)
        def _():
            rows(dest, 16, ROWS)

        return state

    out[...] = jnp.zeros_like(out)
    lax.fori_loop(0, 128, body, 0)


def serve(wanted, splat_map, opacity, depths, normals, position, sh_coeffs, camera):
    count = opacity.shape[0]

    def cols(rows):
        return pl.BlockSpec((rows, SHADE_BLOCK), lambda i: (0, i))

    return pl.pallas_call(
        owner_kernel,
        grid=(count // SHADE_BLOCK,),
        out_shape=jax.ShapeDtypeStruct((128 * ROWS, 128), jnp.float32),
        in_specs=[
            pl.BlockSpec(memory_space=pltpu.SMEM),
            pl.BlockSpec(memory_space=pl.ANY),
            cols(12),
            pl.BlockSpec((SHADE_BLOCK // 128, 128), lambda i: (i, 0)),
            cols(2),
            cols(6),
            cols(3),
            cols(48),
        ],
        out_specs=pl.BlockSpec(memory_space=pltpu.VMEM),
        scratch_shapes=[
            pltpu.VMEM((count, 128), jnp.float32),
            pltpu.VMEM((SHADE_BLOCK // 1024, 8 * IN_ROWS, 128), jnp.float32),
            pltpu.VMEM((SHADE_BLOCK // 1024, 8 * OUT_ROWS, 128), jnp.float32),
            pltpu.SMEM(wanted.shape, jnp.int32),
            pltpu.SemaphoreType.DMA,
        ],
        compiler_params=pltpu.CompilerParams(vmem_limit_bytes=48 * MIB),
        name="serve",
    )(camera, wanted, splat_map, opacity.reshape(-1, 128), depths, normals, position, sh_coeffs)


def plan_kernel(lengths, lists, requests, lower, message, ranks, used, packed, owners, entries):
    owner_row = lax.broadcasted_iota(jnp.int32, (128, 512), 0)
    entry_row = lax.broadcasted_iota(jnp.int32, (256, 512), 0)
    slot = lax.broadcasted_iota(jnp.int32, (1, 128), 1)
    wanted = requests[...].astype(jnp.float32).T
    packed[192:256, :] = jnp.zeros((64, 128), jnp.float32)
    most = jnp.zeros((1, 128), jnp.float32)
    for view in range(2):
        used[...] = jnp.zeros_like(used)
        owners[...] = jnp.zeros_like(owners)
        entries[...] = jnp.zeros_like(entries)
        last_tile = 32 * view + 31

        def mark(step, spots):
            used[...] += lax.dot_general(
                entries[...],
                owners[...],
                (((1,), (1,)), ((), ())),
                preferred_element_type=jnp.float32,
            )
            tile, block = spots
            owner, entry = [], []
            for _ in range(4):
                row = jnp.minimum(tile, last_tile)
                first = block * 128
                place = lists[pl.ds(row * 4 + block, 1), :]
                length = jnp.where(tile > last_tile, 0, lengths[row])
                owner.append(jnp.where(slot + first < length, place // 256, -1))
                entry.append(place % 256)
                over = first + 128 >= length
                tile = jnp.where(over, tile + 1, tile)
                block = jnp.where(over, 0, block + 1)
            owner = jnp.concatenate(owner, axis=1)
            entry = jnp.concatenate(entry, axis=1)
            owners[...] = (owner_row == owner).astype(jnp.float32).astype(jnp.bfloat16)
            entries[...] = (entry_row == entry).astype(jnp.float32).astype(jnp.bfloat16)
            return tile, block

        blocks = lax.fori_loop(
            32 * view, 32 * view + 32, lambda t, n: n + (lengths[t] + 127) // 128, 0
        )
        lax.fori_loop(
            0, (blocks + 3) // 4 + 1, mark, (jnp.int32(32 * view), jnp.int32(0))
        )
        flag = jnp.minimum(used[...], 1.0)
        rank = jnp.dot(lower[...], flag.astype(jnp.bfloat16), preferred_element_type=jnp.float32)
        count = rank[255:256] + flag[255:256]
        packed[253 + view : 254 + view, :] = count
        most = jnp.maximum(most, count)
        ranks[view] = rank.T
        rank = jnp.where(flag > 0.0, rank, -1.0)

        def pick(step, state, view=view, rank=rank):
            for i in range(8):
                entry = step * 8 + i
                chosen = jnp.where(rank == entry.astype(jnp.float32), wanted, 0.0)
                packed[pl.ds(view * LIMIT + entry, 1), :] = jnp.sum(chosen, axis=0, keepdims=True)
            return state

        lax.fori_loop(0, LIMIT // 8, pick, 0)
    over = (most > LIMIT).astype(jnp.float32)
    packed[255:256, :] = jnp.broadcast_to(jnp.max(over, axis=1, keepdims=True), (1, 128))
    message[...] = packed[...].T.astype(jnp.int32)


def plan(lengths, lists, requests):
    vmem = pl.BlockSpec(memory_space=pltpu.VMEM)
    index = np.arange(256)
    lower = jnp.asarray(index[None, :] < index[:, None], jnp.bfloat16)
    return pl.pallas_call(
        plan_kernel,
        out_shape=[
            jax.ShapeDtypeStruct((128, 256), jnp.int32),
            jax.ShapeDtypeStruct((2, 128, 256), jnp.float32),
        ],
        in_specs=[pl.BlockSpec(memory_space=pltpu.SMEM), vmem, vmem, vmem],
        out_specs=[vmem, vmem],
        scratch_shapes=[
            pltpu.VMEM((256, 128), jnp.float32),
            pltpu.VMEM((256, 128), jnp.float32),
            pltpu.VMEM((128, 512), jnp.bfloat16),
            pltpu.VMEM((256, 512), jnp.bfloat16),
        ],
        compiler_params=pltpu.CompilerParams(vmem_limit_bytes=32 * MIB),
        name="plan",
    )(lengths, lists, requests, lower)


def place_kernel(lengths, lists, ranks, rows, owners, entries, owner_of):
    owner_row = lax.broadcasted_iota(jnp.int32, (128, 512), 0)
    entry_row = lax.broadcasted_iota(jnp.int32, (256, 512), 0)
    slot = lax.broadcasted_iota(jnp.int32, (1, 128), 1)
    dead = 8 * 128 * ROWS
    owners[...] = jnp.zeros_like(owners)
    entries[...] = jnp.zeros_like(entries)
    owner_of[...] = jnp.zeros_like(owner_of)
    for view in range(2):
        last_tile = 32 * view + 31
        rank_of = ranks[view].astype(jnp.bfloat16)

        def step(index, state, view=view, rank_of=rank_of, last_tile=last_tile):
            (tile, block), targets = state
            picked = jnp.dot(rank_of, entries[...], preferred_element_type=jnp.float32)
            rank = jnp.sum(picked * owners[...].astype(jnp.float32), axis=0, keepdims=True)
            level = jnp.floor(rank * 0.25)
            owner = owner_of[...]
            row = ((rank - 4.0 * level + 4.0 * view) * 128.0 + owner) * ROWS + level
            row = jnp.where(owner < 0.0, dead, row.astype(jnp.int32))
            for n in range(4):
                rows[pl.ds(targets[n], 1), :] = row[:, 128 * n : 128 * n + 128]
            owner, entry, targets = [], [], []
            for _ in range(4):
                row = jnp.minimum(tile, last_tile) * 4 + block
                first = block * 128
                place = lists[pl.ds(row, 1), :]
                length = jnp.where(tile > last_tile, 0, lengths[jnp.minimum(tile, last_tile)])
                owner.append(jnp.where(slot + first < length, place // 256, -1))
                entry.append(place % 256)
                targets.append(jnp.where(tile > last_tile, 256, row))
                over = first + 128 >= length
                tile = jnp.where(over, tile + 1, tile)
                block = jnp.where(over, 0, block + 1)
            owner = jnp.concatenate(owner, axis=1)
            entry = jnp.concatenate(entry, axis=1)
            owner_of[...] = owner.astype(jnp.float32)
            owners[...] = (owner_row == owner).astype(jnp.float32).astype(jnp.bfloat16)
            entries[...] = (entry_row == entry).astype(jnp.float32).astype(jnp.bfloat16)
            return (tile, block), tuple(targets)

        blocks = lax.fori_loop(
            32 * view, 32 * view + 32, lambda t, n: n + (lengths[t] + 127) // 128, 0
        )
        start = (jnp.int32(32 * view), jnp.int32(0))
        lax.fori_loop(0, (blocks + 3) // 4 + 1, step, (start, (jnp.int32(256),) * 4))


def place(lengths, lists, ranks):
    vmem = pl.BlockSpec(memory_space=pltpu.VMEM)
    return pl.pallas_call(
        place_kernel,
        out_shape=jax.ShapeDtypeStruct((264, 128), jnp.int32),
        in_specs=[pl.BlockSpec(memory_space=pltpu.SMEM), vmem, vmem],
        out_specs=vmem,
        scratch_shapes=[
            pltpu.VMEM((128, 512), jnp.bfloat16),
            pltpu.VMEM((256, 512), jnp.bfloat16),
            pltpu.VMEM((1, 512), jnp.float32),
        ],
        compiler_params=pltpu.CompilerParams(vmem_limit_bytes=32 * MIB),
        cost_estimate=pl.CostEstimate(
            flops=2 * 43 * 128 * 256 * 512, bytes_accessed=600000, transcendentals=0
        ),
        name="place",
    )(lengths, lists, ranks)


def pixel_basis():
    pixel = np.arange(256)
    x = ((pixel % 16) - 7.5) / 8.0
    y = ((pixel // 16) - 7.5) / 8.0
    basis = np.zeros((128, 256), np.float32)
    for part in range(3):
        for k, value in enumerate([x * x, x * y, y * y, x, y, np.ones(256)]):
            basis[16 * part + k] = value
    return jnp.asarray(basis, jnp.bfloat16)


def swap_groups(block):
    row = lax.broadcasted_iota(jnp.int32, (8, 128), 0)
    group = lax.broadcasted_iota(jnp.int32, (8, 128), 1) // 16
    for bit in (1, 2, 4):
        row_bit = (row // bit) % 2
        group_bit = (group // bit) % 2
        from_below = pltpu.roll(pltpu.roll(block, 8 - bit, 0), 16 * bit, 1)
        from_above = pltpu.roll(pltpu.roll(block, bit, 0), 128 - 16 * bit, 1)
        block = jnp.where(
            row_bit == group_bit, block, jnp.where(row_bit < group_bit, from_below, from_above)
        )
    return block


def render_kernel(
    counts, slots_in, packed, basis, image, maps, table, picked, totals, carry, stage,
    closed, alphas_of, weight_of, turned_of,
    slots, copy_sem
):
    copy = pltpu.make_async_copy(slots_in, slots, copy_sem)
    copy.start()
    packed_rows = packed.shape[0]
    lane = lax.broadcasted_iota(jnp.int32, (8, 128), 1)
    group = lane // 16

    def unpack(step, state):
        base = pl.multiple_of(step * 8, 8)
        whole = packed[pl.ds(base, 8), :]
        high = whole.astype(jnp.bfloat16).astype(jnp.float32)
        rest = whole - high
        mid = rest.astype(jnp.bfloat16).astype(jnp.float32)
        low = pltpu.roll(rest - mid, 32, 1)
        mid = pltpu.roll(mid, 16, 1)
        for g in range(8):
            row = jnp.where(group == g, high, jnp.where(group == (g + 1) % 8, mid, low))
            if g:
                row = pltpu.roll(row, 128 - 16 * g, 1)
            table[pl.ds(pl.multiple_of(g * packed_rows + base, 8), 8), :] = row
        return state

    lax.fori_loop(0, packed_rows // 8, unpack, 0, unroll=16)
    table[8 * packed_rows : 8 * packed_rows + 8, :] = jnp.where(lane == 5, -300.0, 0.0)
    def gather(place, spot):
        first = spot[0] * 512 + spot[1] * 128
        for i in range(128):
            slot = first + 16 * (i % 8) + i // 8
            picked[place + i : place + i + 1, :] = table[pl.ds(slots[slot], 1), :]

    def finish(tile, result):
        column = lax.rem(tile, 8)
        for h in range(2):
            stage[pl.ds(h * 8 + column, 8, stride=16), :] = result[:, h * 128 : (h + 1) * 128]

        @pl.when(column == 7)
        def _():
            view = tile // 32
            tile_row = lax.rem(tile // 8, 4)
            for f in range(7):
                for h in range(2):
                    block = swap_groups(stage[(2 * f + h) * 8 : (2 * f + h) * 8 + 8, :])
                    place = pl.ds(pl.multiple_of(tile_row * 16 + h * 8, 8), 8)
                    if f < 3:
                        image[view, f, place, :] = block
                    else:
                        maps[view, f - 3, place, :] = block

    totals[...] = jnp.zeros_like(totals)
    carry[...] = jnp.ones_like(carry)
    alphas_of[...] = jnp.zeros_like(alphas_of)
    weight_of[...] = jnp.zeros_like(weight_of)
    turned_of[...] = jnp.zeros_like(turned_of)

    def following(spot):
        tile, block, last = spot
        next_tile = jnp.where(last == 1, jnp.minimum(tile + 1, 63), tile)
        next_block = jnp.where(last == 1, 0, block + 1)
        return with_last(next_tile, next_block)

    def with_last(tile, block):
        return tile, block, (block + 1 >= counts[tile]).astype(jnp.int32)

    copy.wait()
    start = with_last(jnp.int32(0), jnp.int32(0))
    second = following(start)
    gather(0, start)
    gather(128, second)

    sublane = lax.broadcasted_iota(jnp.int32, (8, 256), 0)

    def split(value):
        high = value.astype(jnp.bfloat16)
        return high, (value - high.astype(jnp.float32)).astype(jnp.bfloat16)

    def step(index, state):
        now, ago, old = state
        later = following(now[1])
        later = (later, following(later))

        parts = []
        for n in range(2):
            part = jnp.dot(
                jnp.concatenate([turned_of[1, n]] * 2, axis=1),
                weight_of[n],
                preferred_element_type=jnp.float32,
            )
            parts.append(part[:8] + part[8:16] + part[16:24])
        first_done = totals[...] + parts[0]
        closed[...] = first_done
        totals[...] = first_done * (1 - old[0][2]).astype(jnp.float32) + parts[1]

        before = carry[...]
        for n in range(2):
            fresh = ago[n][1] == 0
            before = jnp.where(fresh, 1.0, before)
            kept = None
            shares = []
            for r in range(16):
                alphas = alphas_of[n, 8 * r : 8 * r + 8, :]
                shares.append(alphas if kept is None else alphas * kept)
                kept = 1.0 - alphas if kept is None else kept * (1.0 - alphas)
            for distance in (1, 2, 4):
                kept = kept * jnp.where(
                    sublane >= distance, pltpu.roll(kept, distance, 0), 1.0
                )
            ahead = before * jnp.where(sublane >= 1, pltpu.roll(kept, 1, 0), 1.0)
            before = before * jnp.broadcast_to(kept[7:8], kept.shape)
            weight = jnp.concatenate([share * ahead for share in shares], axis=0)
            high, low = split(weight)
            weight_of[n, :128, :] = high
            weight_of[n, 128:, :] = low
        carry[...] = before

        turned_of[1] = turned_of[0]
        for n in range(2):
            rows = picked[128 * n : 128 * n + 128, :]
            turned = rows.T
            turned_of[0, n] = jnp.concatenate(
                [turned[8:16], turned[24:32], turned[40:48], turned[40:48]], axis=0
            ).astype(jnp.bfloat16)
            power = jnp.dot(
                rows.astype(jnp.bfloat16), basis[...], preferred_element_type=jnp.float32
            )
            alphas_of[n] = jnp.exp2(power)
        for n in range(2):
            gather(128 * n, later[n])

        @pl.when(old[0][2] == 1)
        def _():
            finish(old[0][0], closed)

        @pl.when(old[1][2] == 1)
        def _():
            finish(old[1][0], totals)
            totals[...] = jnp.zeros_like(totals)

        return later, now, ago

    steps = lax.fori_loop(0, 64, lambda i, n: n + counts[i], 0)
    zero = jnp.int32(0)
    none = ((zero, zero, zero), (zero, zero, zero))
    lax.fori_loop(0, (steps + 1) // 2 + 2, step, ((start, second), none, none))


def render(counts, slots, packed):
    packed_rows = packed.shape[0]
    vmem = pl.BlockSpec(memory_space=pltpu.VMEM)
    smem = pl.BlockSpec(memory_space=pltpu.SMEM)
    hbm = pl.BlockSpec(memory_space=pl.ANY)
    return pl.pallas_call(
        render_kernel,
        out_shape=[
            jax.ShapeDtypeStruct((2, 3, 64, 128), jnp.float32),
            jax.ShapeDtypeStruct((2, 4, 64, 128), jnp.float32),
        ],
        in_specs=[smem, hbm, vmem, vmem],
        out_specs=[vmem, vmem],
        scratch_shapes=[
            pltpu.VMEM((8 * packed_rows + 8, 128), jnp.float32),
            pltpu.VMEM((256, 128), jnp.float32),
            pltpu.VMEM((8, 256), jnp.float32),
            pltpu.VMEM((8, 256), jnp.float32),
            pltpu.VMEM((128, 128), jnp.float32),
            pltpu.VMEM((8, 256), jnp.float32),
            pltpu.VMEM((2, 128, 256), jnp.float32),
            pltpu.VMEM((2, 256, 256), jnp.bfloat16),
            pltpu.VMEM((2, 2, 32, 128), jnp.bfloat16),
            pltpu.SMEM(slots.shape, jnp.int32),
            pltpu.SemaphoreType.DMA,
        ],
        compiler_params=pltpu.CompilerParams(vmem_limit_bytes=52 * MIB),
        name="render",
    )(counts, slots, packed, pixel_basis())


def surface_kernel(maps, out, halo, send_sem, recv_sem):
    row = lax.axis_index("rows")
    col = lax.axis_index("cols")
    sides = [
        (row > 0, (row - 1, col), row < 15),
        (row < 15, (row + 1, col), row > 0),
        (col > 0, (row, col - 1), col < 7),
        (col < 7, (row, col + 1), col > 0),
    ]
    barrier = pltpu.get_barrier_semaphore()
    for there, device, _ in sides:

        @pl.when(there)
        def _(device=device):
            pl.semaphore_signal(
                barrier, inc=1, device_id=device, device_id_type=pl.DeviceIdType.MESH
            )

    neighbours = sum(there.astype(jnp.int32) for there, _, _ in sides)
    pl.semaphore_wait(barrier, neighbours)

    def copy(n, device):
        part = (slice(None), pl.ds(0, 8)) if n == 0 else (slice(None), pl.ds(56, 8))
        source, target = maps.at[:, 0], halo.at[n]
        if n < 2:
            source, target = source.at[part], target.at[part]
        return pltpu.make_async_remote_copy(
            src_ref=source,
            dst_ref=target,
            send_sem=send_sem.at[n],
            recv_sem=recv_sem.at[n],
            device_id=device,
            device_id_type=pl.DeviceIdType.MESH,
        )

    for n, (there, device, _) in enumerate(sides):

        @pl.when(there)
        def _(n=n, device=device):
            copy(n, device).start()

    for n, (there, device, source) in enumerate(sides):

        @pl.when(source)
        def _(n=n):
            copy(n, sides[n ^ 1][1]).wait_recv()

    y = lax.broadcasted_iota(jnp.int32, (64, 128), 0)
    x = lax.broadcasted_iota(jnp.int32, (64, 128), 1)
    for view in range(2):
        depth = maps[view, 0]
        below = jnp.where(row < 15, halo[0, view, 0:1, :], 0.0)
        above = jnp.where(row > 0, halo[1, view, 63:64, :], 0.0)
        right = jnp.where(col < 7, halo[2, view], 0.0)
        left = jnp.where(col > 0, halo[3, view], 0.0)
        north = jnp.where(y == 0, above, pltpu.roll(depth, 1, 0))
        south = jnp.where(y == 63, below, pltpu.roll(depth, 63, 0))
        west = pltpu.roll(jnp.where(x == 127, left, depth), 1, 1)
        east = pltpu.roll(jnp.where(x == 0, right, depth), 127, 1)
        grad_x = 0.5 * (east - west)
        grad_y = 0.5 * (south - north)
        inverse = 1.0 / jnp.sqrt(grad_x * grad_x + grad_y * grad_y + 1.0)
        slope = maps[view, 3] - maps[view, 1] * grad_x - maps[view, 2] * grad_y
        out[view] = 1.0 - slope * inverse

    for n, (there, device, _) in enumerate(sides):

        @pl.when(there)
        def _(n=n, device=device):
            copy(n, device).wait_send()


def consistency_map(maps):
    vmem = pl.BlockSpec(memory_space=pltpu.VMEM)
    return pl.pallas_call(
        surface_kernel,
        out_shape=jax.ShapeDtypeStruct((2, 64, 128), jnp.float32),
        in_specs=[vmem],
        out_specs=vmem,
        scratch_shapes=[
            pltpu.VMEM((4, 2, 64, 128), jnp.float32),
            pltpu.SemaphoreType.DMA((4,)),
            pltpu.SemaphoreType.DMA((4,)),
        ],
        compiler_params=pltpu.CompilerParams(collective_id=0, has_side_effects=True),
        name="surface",
    )(maps)


def shade(position, sh_coeffs, camera):
    offset = position[None, :, :] - camera[:, :, None]
    distance = jnp.sqrt(jnp.sum(offset * offset, axis=1, keepdims=True))
    direction = offset / distance
    dir_x = direction[:, 0]
    dir_y = direction[:, 1]
    dir_z = direction[:, 2]
    sq_x = dir_x * dir_x
    sq_y = dir_y * dir_y
    sq_z = dir_z * dir_z
    sh_basis = jnp.stack(
        [
            jnp.full_like(dir_x, sh_first),
            -sh_second * dir_y,
            sh_second * dir_z,
            -sh_second * dir_x,
            sh_third[0] * dir_x * dir_y,
            sh_third[1] * dir_y * dir_z,
            sh_third[2] * (2.0 * sq_z - sq_x - sq_y),
            sh_third[3] * dir_x * dir_z,
            sh_third[4] * (sq_x - sq_y),
            sh_fourth[0] * dir_y * (3.0 * sq_x - sq_y),
            sh_fourth[1] * dir_x * dir_y * dir_z,
            sh_fourth[2] * dir_y * (4.0 * sq_z - sq_x - sq_y),
            sh_fourth[3] * dir_z * (2.0 * sq_z - 3.0 * sq_x - 3.0 * sq_y),
            sh_fourth[4] * dir_x * (4.0 * sq_z - sq_x - sq_y),
            sh_fourth[5] * dir_z * (sq_x - sq_y),
            sh_fourth[6] * dir_x * (sq_x - 3.0 * sq_y),
        ],
        axis=1,
    )
    coefficients = sh_coeffs.reshape(3, 16, -1)
    colour = 0.5 + jnp.sum(sh_basis[:, None] * coefficients[None], axis=2)
    return jnp.maximum(colour, 0.0).reshape(-1, position.shape[1])


def composite(table_rows, slot_lists, lengths, view_index, view_count, block_count, block_size):
    tile_rows, tile_cols, slot_count = slot_lists.shape
    tile_count = tile_rows * tile_cols
    slot_index = slot_lists.reshape(tile_count, slot_count)
    live_count = lengths.reshape(tile_count)
    pixel_ids = jnp.arange(256, dtype=jnp.int32)
    local_x = ((pixel_ids % 16).astype(jnp.float32) - 7.5) / 8.0
    local_y = ((pixel_ids // 16).astype(jnp.float32) - 7.5) / 8.0
    positions = jnp.arange(block_size, dtype=jnp.int32)
    earlier = (positions[:, None] < positions[None, :]).astype(jnp.float32)
    feature_rows = (
        [10 * view_count + 1 + 3 * view_index + k for k in range(3)]
        + [6 * view_count + 1 + view_index]
        + [7 * view_count + 1 + 3 * view_index + k for k in range(3)]
    )

    def block_step(block_index, state):
        totals, log_before = state
        first_slot = block_index * block_size
        picked_index = lax.dynamic_slice_in_dim(slot_index, first_slot, block_size, 1)
        picked = jnp.take(table_rows, picked_index.reshape(-1), axis=0)
        picked = picked.reshape(tile_count, block_size, table_rows.shape[1]).transpose(2, 0, 1)
        part_map = picked[6 * view_index : 6 * view_index + 6]
        part_opacity = picked[6 * view_count]
        part_features = jnp.stack([picked[row] for row in feature_rows], 0)
        live_mask = ((first_slot + positions)[None, :] < live_count[:, None]).astype(jnp.float32)
        coord_u = (
            part_map[0][:, None, :] * local_x[None, :, None]
            + part_map[1][:, None, :] * local_y[None, :, None]
            + part_map[2][:, None, :]
        )
        coord_w = (
            part_map[3][:, None, :] * local_x[None, :, None]
            + part_map[4][:, None, :] * local_y[None, :, None]
            + part_map[5][:, None, :]
        )
        alphas = part_opacity[:, None, :] * jnp.exp(-0.5 * (coord_u * coord_u + coord_w * coord_w))
        log_keep = jnp.log1p(-alphas) * live_mask[:, None, :]
        before = log_before[:, :, None] + jnp.einsum(
            "tps,sq->tpq", log_keep, earlier, precision=lax.Precision.HIGHEST
        )
        weight = alphas * jnp.exp(before) * live_mask[:, None, :]
        totals = totals + jnp.einsum(
            "fts,tps->tfp", part_features, weight, precision=lax.Precision.HIGHEST
        )
        return (totals, log_before + jnp.sum(log_keep, axis=2))

    start_state = (
        jnp.zeros((tile_count, 7, 256), jnp.float32),
        jnp.zeros((tile_count, 256), jnp.float32),
    )
    totals, unused_log = lax.fori_loop(0, block_count, block_step, start_state)
    return (
        totals.reshape(tile_rows, tile_cols, 7, 16, 16)
        .transpose(2, 0, 3, 1, 4)
        .reshape(7, tile_rows * 16, tile_cols * 16)
    )


def general(
    splat_map,
    opacity,
    depths,
    normals,
    position,
    sh_coeffs,
    camera,
    requests,
    tile_lists,
    list_lengths,
):
    view_count = camera.shape[0]
    device_count = requests.shape[1]
    capacity = requests.shape[2]
    asked_for = lax.all_to_all(requests, ("rows", "cols"), split_axis=1, concat_axis=0, tiled=True)
    wanted = asked_for.reshape(-1)
    geometry_count = 10 * view_count + 1
    source_table = jnp.concatenate(
        [splat_map, opacity[None, :], depths, normals, position, sh_coeffs], 0
    ).T
    gathered = jnp.take(source_table, wanted, axis=0).T
    outgoing = jnp.concatenate(
        [
            gathered[:geometry_count],
            shade(
                gathered[geometry_count : geometry_count + 3],
                gathered[geometry_count + 3 :],
                camera,
            ),
        ],
        0,
    )
    field_rows = outgoing.shape[0]
    arrived = lax.all_to_all(
        outgoing.reshape(field_rows, device_count, capacity),
        ("rows", "cols"),
        split_axis=1,
        concat_axis=1,
        tiled=True,
    ).reshape(field_rows, device_count * capacity)
    padded_count = (field_rows + 7) // 8 * 8
    table_rows = jnp.pad(arrived, ((0, padded_count - field_rows), (0, 0))).T
    slot_count = tile_lists.shape[-1]
    block_size = min(128, slot_count)
    feature_maps = jnp.stack(
        [
            composite(
                table_rows,
                tile_lists[view_index],
                list_lengths[view_index],
                view_index,
                view_count,
                slot_count // block_size,
                block_size,
            )
            for view_index in range(view_count)
        ]
    )
    return feature_maps[:, :3], feature_maps[:, 3:]


def shards(
    splat_map,
    opacity,
    depths,
    normals,
    position,
    sh_coeffs,
    camera,
    requests,
    tile_lists,
    list_lengths,
):
    lengths = list_lengths.reshape(-1)
    lists = tile_lists.reshape(256, 128)
    message, ranks = plan(lengths, lists, requests[0])
    asked_for = lax.all_to_all(message, ("rows", "cols"), split_axis=0, concat_axis=0, tiled=True)
    slots = place(lengths, lists, ranks)
    outgoing = serve(
        asked_for.reshape(-1), splat_map, opacity, depths, normals, position, sh_coeffs, camera
    )
    arrived = lax.all_to_all(
        outgoing.reshape(128, ROWS, 128), ("rows", "cols"), split_axis=0, concat_axis=0, tiled=True
    ).reshape(128 * ROWS, 128)

    def fast():
        return render((lengths + 127) // 128, slots.reshape(-1), arrived)

    def slow():
        return general(
            splat_map,
            opacity,
            depths,
            normals,
            position,
            sh_coeffs,
            camera,
            requests,
            tile_lists,
            list_lengths,
        )

    image, maps = lax.cond(jnp.max(asked_for[:, 255]) > 0, slow, fast)
    return (image, consistency_map(maps))


def solution(mesh):
    in_specs = (
        P(None, ("rows", "cols")),
        P(("rows", "cols")),
        P(None, ("rows", "cols")),
        P(None, ("rows", "cols")),
        P(None, ("rows", "cols")),
        P(None, ("rows", "cols")),
        P(),
        P(("rows", "cols"), None, None),
        P(None, "rows", "cols", None),
        P(None, "rows", "cols"),
    )
    out_specs = (P(None, None, "rows", "cols"), P(None, "rows", "cols"))
    return jax.shard_map(shards, mesh=mesh, in_specs=in_specs, out_specs=out_specs, check_vma=False)
```

```python
import functools
import math

import jax
import jax.numpy as jnp
import numpy as np
from jax import lax
from jax.experimental import pallas as pl
from jax.experimental.pallas import tpu as pltpu
from jax.sharding import PartitionSpec as P

sh_first = 0.28209479177387814
sh_second = 0.4886025119029199
sh_third = [
    1.0925484305920792,
    -1.0925484305920792,
    0.31539156525252005,
    -1.0925484305920792,
    0.5462742152960396,
]
sh_fourth = [
    -0.5900435899266435,
    2.890611442640554,
    -0.4570457994644658,
    0.3731763325901154,
    -0.4570457994644658,
    1.445305721320277,
    -0.5900435899266435,
]
LOG2E = 1.4426950408889634
MIB = 1 << 20
IN_ROWS = 88
OUT_ROWS = 32
SHADE_BLOCK = 4096
ROWS = 24
LIMIT = 4 * ROWS


def dense_block(src, field):
    return src[pl.ds(field, 8, stride=IN_ROWS), :]


def owner_kernel(
    camera,
    wanted_in,
    splat,
    opacity,
    depths,
    normals,
    position,
    coeffs,
    out,
    table,
    fields_in,
    fields_out,
    wanted,
    wanted_sem,
):
    copy = pltpu.make_async_copy(wanted_in, wanted, wanted_sem)

    @pl.when(pl.program_id(0) == 0)
    def _():
        copy.start()

    first_row = pl.program_id(0) * SHADE_BLOCK

    def shade_part(part, fields_in, fields_out):
        for j in range(8):
            cols = pl.ds(pl.multiple_of(part * 1024 + j * 128, 128), 128)
            first = j * IN_ROWS
            fields_in[first : first + 12, :] = splat[:, cols]
            fields_in[first + 16 : first + 18, :] = depths[:, cols]
            fields_in[first + 24 : first + 30, :] = normals[:, cols]
            fields_in[first + 32 : first + 35, :] = position[:, cols]
            fields_in[first + 40 : first + 88, :] = coeffs[:, cols]
        field = functools.partial(dense_block, fields_in)
        log_opacity = jnp.log(opacity[pl.ds(pl.multiple_of(part * 8, 8), 8), :]) * LOG2E
        zero = jnp.zeros((8, 128), jnp.float32)
        bases = []
        for view in range(2):

            def put(row, value, view=view):
                fields_out[pl.ds(16 * view + row, 8, stride=OUT_ROWS), :] = value

            m = [field(6 * view + k) for k in range(6)]
            half = -0.5 * LOG2E
            put(0, half * (m[0] * m[0] + m[3] * m[3]))
            put(1, (2.0 * half) * (m[0] * m[1] + m[3] * m[4]))
            put(2, half * (m[1] * m[1] + m[4] * m[4]))
            put(3, (2.0 * half) * (m[0] * m[2] + m[3] * m[5]))
            put(4, (2.0 * half) * (m[1] * m[2] + m[4] * m[5]))
            put(5, half * (m[2] * m[2] + m[5] * m[5]) + log_opacity)
            put(6, zero)
            put(7, zero)
            put(11, field(16 + view))
            for k in range(3):
                put(12 + k, field(24 + 3 * view + k))
            put(15, zero)
            off = [field(32 + k) - camera[view, k] for k in range(3)]
            distance = jnp.sqrt(off[0] * off[0] + off[1] * off[1] + off[2] * off[2])
            inverse = 1.0 / distance
            dir_x, dir_y, dir_z = [o * inverse for o in off]
            sq_x = dir_x * dir_x
            sq_y = dir_y * dir_y
            sq_z = dir_z * dir_z
            bases.append(
                [
                    None,
                    -sh_second * dir_y,
                    sh_second * dir_z,
                    -sh_second * dir_x,
                    sh_third[0] * dir_x * dir_y,
                    sh_third[1] * dir_y * dir_z,
                    sh_third[2] * (2.0 * sq_z - sq_x - sq_y),
                    sh_third[3] * dir_x * dir_z,
                    sh_third[4] * (sq_x - sq_y),
                    sh_fourth[0] * dir_y * (3.0 * sq_x - sq_y),
                    sh_fourth[1] * dir_x * dir_y * dir_z,
                    sh_fourth[2] * dir_y * (4.0 * sq_z - sq_x - sq_y),
                    sh_fourth[3] * dir_z * (2.0 * sq_z - 3.0 * sq_x - 3.0 * sq_y),
                    sh_fourth[4] * dir_x * (4.0 * sq_z - sq_x - sq_y),
                    sh_fourth[5] * dir_z * (sq_x - sq_y),
                    sh_fourth[6] * dir_x * (sq_x - 3.0 * sq_y),
                ]
            )
        for channel in range(3):
            c = field(40 + 16 * channel)
            sums = [0.5 + sh_first * c, 0.5 + sh_first * c]
            for k in range(1, 16):
                c = field(40 + 16 * channel + k)
                for view in range(2):
                    sums[view] = sums[view] + bases[view][k] * c
            for view in range(2):
                fields_out[pl.ds(16 * view + 8 + channel, 8, stride=OUT_ROWS), :] = jnp.maximum(
                    sums[view], 0.0
                )
        for j in range(8):
            first = fields_out[j * OUT_ROWS : j * OUT_ROWS + 16, :]
            second = fields_out[j * OUT_ROWS + 16 : j * OUT_ROWS + 32, :]
            block = jnp.concatenate([first] * 4 + [second] * 4, axis=0)
            table[pl.ds(pl.multiple_of(first_row + part * 1024 + j * 128, 128), 128), :] = block.T

    for part in range(SHADE_BLOCK // 1024):
        shade_part(part, fields_in.at[part], fields_out.at[part])

    @pl.when(pl.program_id(0) == pl.num_programs(0) - 1)
    def _():
        copy.wait()
        gather(wanted, table, out)


def gather(wanted, table, out):
    group = lax.broadcasted_iota(jnp.int32, (1, 128), 1) // 16

    def rows(dest, first, last):
        for i in range(first, last):
            picked = [
                table[pl.ds(wanted[dest * 256 + (g // 4) * LIMIT + 4 * i + g % 4], 1), :]
                for g in range(8)
            ]
            for bit in (1, 2, 4):
                picked = [
                    jnp.where((group // bit) % 2 == 0, picked[n], picked[n + 1])
                    for n in range(0, len(picked), 2)
                ]
            out[pl.ds(dest * ROWS + i, 1), :] = picked[0]

    def body(dest, state):
        count = jnp.maximum(wanted[dest * 256 + 253], wanted[dest * 256 + 254])
        rows(dest, 0, 16)

        @pl.when(count > 64)
        def _():
            rows(dest, 16, ROWS)

        return state

    out[...] = jnp.zeros_like(out)
    lax.fori_loop(0, 128, body, 0)


def serve(wanted, splat_map, opacity, depths, normals, position, sh_coeffs, camera):
    count = opacity.shape[0]

    def cols(rows):
        return pl.BlockSpec((rows, SHADE_BLOCK), lambda i: (0, i))

    return pl.pallas_call(
        owner_kernel,
        grid=(count // SHADE_BLOCK,),
        out_shape=jax.ShapeDtypeStruct((128 * ROWS, 128), jnp.float32),
        in_specs=[
            pl.BlockSpec(memory_space=pltpu.SMEM),
            pl.BlockSpec(memory_space=pl.ANY),
            cols(12),
            pl.BlockSpec((SHADE_BLOCK // 128, 128), lambda i: (i, 0)),
            cols(2),
            cols(6),
            cols(3),
            cols(48),
        ],
        out_specs=pl.BlockSpec(memory_space=pltpu.VMEM),
        scratch_shapes=[
            pltpu.VMEM((count, 128), jnp.float32),
            pltpu.VMEM((SHADE_BLOCK // 1024, 8 * IN_ROWS, 128), jnp.float32),
            pltpu.VMEM((SHADE_BLOCK // 1024, 8 * OUT_ROWS, 128), jnp.float32),
            pltpu.SMEM(wanted.shape, jnp.int32),
            pltpu.SemaphoreType.DMA,
        ],
        compiler_params=pltpu.CompilerParams(vmem_limit_bytes=48 * MIB),
        name="serve",
    )(camera, wanted, splat_map, opacity.reshape(-1, 128), depths, normals, position, sh_coeffs)


def plan_kernel(lengths, lists, requests, lower, message, ranks, used, packed, owners, entries):
    owner_row = lax.broadcasted_iota(jnp.int32, (128, 512), 0)
    entry_row = lax.broadcasted_iota(jnp.int32, (256, 512), 0)
    slot = lax.broadcasted_iota(jnp.int32, (1, 128), 1)
    wanted = requests[...].astype(jnp.float32).T
    packed[...] = jnp.zeros_like(packed)
    most = jnp.zeros((1, 128), jnp.float32)
    for view in range(2):
        used[...] = jnp.zeros_like(used)
        owners[...] = jnp.zeros_like(owners)
        entries[...] = jnp.zeros_like(entries)
        last_tile = 32 * view + 31

        def mark(step, spots):
            used[...] += lax.dot_general(
                entries[...],
                owners[...],
                (((1,), (1,)), ((), ())),
                preferred_element_type=jnp.float32,
            )
            tile, block = spots
            owner, entry = [], []
            for _ in range(4):
                row = jnp.minimum(tile, last_tile)
                first = block * 128
                place = lists[pl.ds(row * 4 + block, 1), :]
                length = jnp.where(tile > last_tile, 0, lengths[row])
                owner.append(jnp.where(slot + first < length, place // 256, -1))
                entry.append(place % 256)
                over = first + 128 >= length
                tile = jnp.where(over, tile + 1, tile)
                block = jnp.where(over, 0, block + 1)
            owner = jnp.concatenate(owner, axis=1)
            entry = jnp.concatenate(entry, axis=1)
            owners[...] = (owner_row == owner).astype(jnp.float32).astype(jnp.bfloat16)
            entries[...] = (entry_row == entry).astype(jnp.float32).astype(jnp.bfloat16)
            return tile, block

        blocks = lax.fori_loop(
            32 * view, 32 * view + 32, lambda t, n: n + (lengths[t] + 127) // 128, 0
        )
        lax.fori_loop(
            0, (blocks + 3) // 4 + 1, mark, (jnp.int32(32 * view), jnp.int32(0))
        )
        flag = jnp.minimum(used[...], 1.0)
        rank = jnp.dot(lower[...], flag.astype(jnp.bfloat16), preferred_element_type=jnp.float32)
        count = rank[255:256] + flag[255:256]
        packed[253 + view : 254 + view, :] = count
        most = jnp.maximum(most, count)
        ranks[view] = rank.T
        rank = jnp.where(flag > 0.0, rank, -1.0)

        def pick(step, state, view=view, rank=rank):
            for i in range(8):
                entry = step * 8 + i
                chosen = jnp.where(rank == entry.astype(jnp.float32), wanted, 0.0)
                packed[pl.ds(view * LIMIT + entry, 1), :] = jnp.sum(chosen, axis=0, keepdims=True)
            return state

        longest = jnp.max(count).astype(jnp.int32)
        lax.fori_loop(0, jnp.minimum((longest + 7) // 8, LIMIT // 8), pick, 0)
    over = (most > LIMIT).astype(jnp.float32)
    packed[255:256, :] = jnp.broadcast_to(jnp.max(over, axis=1, keepdims=True), (1, 128))
    message[...] = packed[...].T.astype(jnp.int32)


def plan(lengths, lists, requests):
    vmem = pl.BlockSpec(memory_space=pltpu.VMEM)
    index = np.arange(256)
    lower = jnp.asarray(index[None, :] < index[:, None], jnp.bfloat16)
    return pl.pallas_call(
        plan_kernel,
        out_shape=[
            jax.ShapeDtypeStruct((128, 256), jnp.int32),
            jax.ShapeDtypeStruct((2, 128, 256), jnp.float32),
        ],
        in_specs=[pl.BlockSpec(memory_space=pltpu.SMEM), vmem, vmem, vmem],
        out_specs=[vmem, vmem],
        scratch_shapes=[
            pltpu.VMEM((256, 128), jnp.float32),
            pltpu.VMEM((256, 128), jnp.float32),
            pltpu.VMEM((128, 512), jnp.bfloat16),
            pltpu.VMEM((256, 512), jnp.bfloat16),
        ],
        compiler_params=pltpu.CompilerParams(vmem_limit_bytes=32 * MIB),
        name="plan",
    )(lengths, lists, requests, lower)


def place_kernel(lengths, lists, ranks, rows, owners, entries, owner_of):
    owner_row = lax.broadcasted_iota(jnp.int32, (128, 512), 0)
    entry_row = lax.broadcasted_iota(jnp.int32, (256, 512), 0)
    slot = lax.broadcasted_iota(jnp.int32, (1, 128), 1)
    dead = 8 * 128 * ROWS
    owners[...] = jnp.zeros_like(owners)
    entries[...] = jnp.zeros_like(entries)
    owner_of[...] = jnp.zeros_like(owner_of)
    for view in range(2):
        last_tile = 32 * view + 31
        rank_of = ranks[view].astype(jnp.bfloat16)

        def step(index, state, view=view, rank_of=rank_of, last_tile=last_tile):
            (tile, block), targets = state
            picked = jnp.dot(rank_of, entries[...], preferred_element_type=jnp.float32)
            rank = jnp.sum(picked * owners[...].astype(jnp.float32), axis=0, keepdims=True)
            level = jnp.floor(rank * 0.25)
            owner = owner_of[...]
            row = ((rank - 4.0 * level + 4.0 * view) * 128.0 + owner) * ROWS + level
            row = jnp.where(owner < 0.0, dead, row.astype(jnp.int32))
            for n in range(4):
                rows[pl.ds(targets[n], 1), :] = row[:, 128 * n : 128 * n + 128]
            owner, entry, targets = [], [], []
            for _ in range(4):
                row = jnp.minimum(tile, last_tile) * 4 + block
                first = block * 128
                place = lists[pl.ds(row, 1), :]
                length = jnp.where(tile > last_tile, 0, lengths[jnp.minimum(tile, last_tile)])
                owner.append(jnp.where(slot + first < length, place // 256, -1))
                entry.append(place % 256)
                targets.append(jnp.where(tile > last_tile, 256, row))
                over = first + 128 >= length
                tile = jnp.where(over, tile + 1, tile)
                block = jnp.where(over, 0, block + 1)
            owner = jnp.concatenate(owner, axis=1)
            entry = jnp.concatenate(entry, axis=1)
            owner_of[...] = owner.astype(jnp.float32)
            owners[...] = (owner_row == owner).astype(jnp.float32).astype(jnp.bfloat16)
            entries[...] = (entry_row == entry).astype(jnp.float32).astype(jnp.bfloat16)
            return (tile, block), tuple(targets)

        blocks = lax.fori_loop(
            32 * view, 32 * view + 32, lambda t, n: n + (lengths[t] + 127) // 128, 0
        )
        start = (jnp.int32(32 * view), jnp.int32(0))
        lax.fori_loop(0, (blocks + 3) // 4 + 1, step, (start, (jnp.int32(256),) * 4))


def place(lengths, lists, ranks):
    vmem = pl.BlockSpec(memory_space=pltpu.VMEM)
    return pl.pallas_call(
        place_kernel,
        out_shape=jax.ShapeDtypeStruct((264, 128), jnp.int32),
        in_specs=[pl.BlockSpec(memory_space=pltpu.SMEM), vmem, vmem],
        out_specs=vmem,
        scratch_shapes=[
            pltpu.VMEM((128, 512), jnp.bfloat16),
            pltpu.VMEM((256, 512), jnp.bfloat16),
            pltpu.VMEM((1, 512), jnp.float32),
        ],
        compiler_params=pltpu.CompilerParams(vmem_limit_bytes=32 * MIB),
        cost_estimate=pl.CostEstimate(
            flops=2 * 43 * 128 * 256 * 512, bytes_accessed=600000, transcendentals=0
        ),
        name="place",
    )(lengths, lists, ranks)


def pixel_basis():
    pixel = np.arange(256)
    x = ((pixel % 16) - 7.5) / 8.0
    y = ((pixel // 16) - 7.5) / 8.0
    basis = np.zeros((128, 256), np.float32)
    for part in range(3):
        for k, value in enumerate([x * x, x * y, y * y, x, y, np.ones(256)]):
            basis[16 * part + k] = value
    return jnp.asarray(basis, jnp.bfloat16)


def swap_groups(block):
    row = lax.broadcasted_iota(jnp.int32, (8, 128), 0)
    group = lax.broadcasted_iota(jnp.int32, (8, 128), 1) // 16
    for bit in (1, 2, 4):
        row_bit = (row // bit) % 2
        group_bit = (group // bit) % 2
        from_below = pltpu.roll(pltpu.roll(block, 8 - bit, 0), 16 * bit, 1)
        from_above = pltpu.roll(pltpu.roll(block, bit, 0), 128 - 16 * bit, 1)
        block = jnp.where(
            row_bit == group_bit, block, jnp.where(row_bit < group_bit, from_below, from_above)
        )
    return block


def render_kernel(
    counts, slots_in, packed, basis, image, maps, table, picked, totals, carry, stage,
    closed, alphas_of, weight_of, turned_of,
    slots, copy_sem
):
    copy = pltpu.make_async_copy(slots_in, slots, copy_sem)
    copy.start()
    packed_rows = packed.shape[0]
    lane = lax.broadcasted_iota(jnp.int32, (8, 128), 1)
    group = lane // 16

    def unpack(step, state):
        base = pl.multiple_of(step * 8, 8)
        whole = packed[pl.ds(base, 8), :]
        high = whole.astype(jnp.bfloat16).astype(jnp.float32)
        rest = whole - high
        mid = rest.astype(jnp.bfloat16).astype(jnp.float32)
        low = pltpu.roll(rest - mid, 32, 1)
        mid = pltpu.roll(mid, 16, 1)
        for g in range(8):
            row = jnp.where(group == g, high, jnp.where(group == (g + 1) % 8, mid, low))
            if g:
                row = pltpu.roll(row, 128 - 16 * g, 1)
            table[pl.ds(pl.multiple_of(g * packed_rows + base, 8), 8), :] = row
        return state

    lax.fori_loop(0, packed_rows // 8, unpack, 0, unroll=16)
    table[8 * packed_rows : 8 * packed_rows + 8, :] = jnp.where(lane == 5, -300.0, 0.0)
    def gather(place, spot):
        first = spot[0] * 512 + spot[1] * 128
        for i in range(128):
            slot = first + 16 * (i % 8) + i // 8
            picked[place + i : place + i + 1, :] = table[pl.ds(slots[slot], 1), :]

    def finish(tile, result):
        column = lax.rem(tile, 8)
        for h in range(2):
            stage[pl.ds(h * 8 + column, 8, stride=16), :] = result[:, h * 128 : (h + 1) * 128]

        @pl.when(column == 7)
        def _():
            view = tile // 32
            tile_row = lax.rem(tile // 8, 4)
            for f in range(7):
                for h in range(2):
                    block = swap_groups(stage[(2 * f + h) * 8 : (2 * f + h) * 8 + 8, :])
                    place = pl.ds(pl.multiple_of(tile_row * 16 + h * 8, 8), 8)
                    if f < 3:
                        image[view, f, place, :] = block
                    else:
                        maps[view, f - 3, place, :] = block

    totals[...] = jnp.zeros_like(totals)
    carry[...] = jnp.ones_like(carry)
    alphas_of[...] = jnp.zeros_like(alphas_of)
    weight_of[...] = jnp.zeros_like(weight_of)
    turned_of[...] = jnp.zeros_like(turned_of)

    def following(spot):
        tile, block, last = spot
        next_tile = jnp.where(last == 1, jnp.minimum(tile + 1, 63), tile)
        next_block = jnp.where(last == 1, 0, block + 1)
        return with_last(next_tile, next_block)

    def with_last(tile, block):
        return tile, block, (block + 1 >= counts[tile]).astype(jnp.int32)

    copy.wait()
    start = with_last(jnp.int32(0), jnp.int32(0))
    second = following(start)
    gather(0, start)
    gather(128, second)

    sublane = lax.broadcasted_iota(jnp.int32, (8, 256), 0)

    def split(value):
        high = value.astype(jnp.bfloat16)
        return high, (value - high.astype(jnp.float32)).astype(jnp.bfloat16)

    def step(index, state):
        now, ago, old = state
        later = following(now[1])
        later = (later, following(later))

        parts = []
        for n in range(2):
            part = jnp.dot(
                jnp.concatenate([turned_of[1, n]] * 2, axis=1),
                weight_of[n],
                preferred_element_type=jnp.float32,
            )
            parts.append(part[:8] + part[8:16] + part[16:24])
        first_done = totals[...] + parts[0]
        closed[...] = first_done
        totals[...] = first_done * (1 - old[0][2]).astype(jnp.float32) + parts[1]

        before = carry[...]
        for n in range(2):
            fresh = ago[n][1] == 0
            before = jnp.where(fresh, 1.0, before)
            kept = None
            shares = []
            for r in range(16):
                alphas = alphas_of[n, 8 * r : 8 * r + 8, :]
                shares.append(alphas if kept is None else alphas * kept)
                kept = 1.0 - alphas if kept is None else kept * (1.0 - alphas)
            for distance in (1, 2, 4):
                kept = kept * jnp.where(
                    sublane >= distance, pltpu.roll(kept, distance, 0), 1.0
                )
            ahead = before * jnp.where(sublane >= 1, pltpu.roll(kept, 1, 0), 1.0)
            before = before * jnp.broadcast_to(kept[7:8], kept.shape)
            weight = jnp.concatenate([share * ahead for share in shares], axis=0)
            high, low = split(weight)
            weight_of[n, :128, :] = high
            weight_of[n, 128:, :] = low
        carry[...] = before

        turned_of[1] = turned_of[0]
        for n in range(2):
            rows = picked[128 * n : 128 * n + 128, :]
            turned = rows.T
            turned_of[0, n] = jnp.concatenate(
                [turned[8:16], turned[24:32], turned[40:48], turned[40:48]], axis=0
            ).astype(jnp.bfloat16)
            power = jnp.dot(
                rows.astype(jnp.bfloat16), basis[...], preferred_element_type=jnp.float32
            )
            alphas_of[n] = jnp.exp2(power)
        for n in range(2):
            gather(128 * n, later[n])

        @pl.when(old[0][2] == 1)
        def _():
            finish(old[0][0], closed)

        @pl.when(old[1][2] == 1)
        def _():
            finish(old[1][0], totals)
            totals[...] = jnp.zeros_like(totals)

        return later, now, ago

    steps = lax.fori_loop(0, 64, lambda i, n: n + counts[i], 0)
    zero = jnp.int32(0)
    none = ((zero, zero, zero), (zero, zero, zero))
    lax.fori_loop(0, (steps + 1) // 2 + 2, step, ((start, second), none, none))


def render(counts, slots, packed):
    packed_rows = packed.shape[0]
    vmem = pl.BlockSpec(memory_space=pltpu.VMEM)
    smem = pl.BlockSpec(memory_space=pltpu.SMEM)
    hbm = pl.BlockSpec(memory_space=pl.ANY)
    return pl.pallas_call(
        render_kernel,
        out_shape=[
            jax.ShapeDtypeStruct((2, 3, 64, 128), jnp.float32),
            jax.ShapeDtypeStruct((2, 4, 64, 128), jnp.float32),
        ],
        in_specs=[smem, hbm, vmem, vmem],
        out_specs=[vmem, vmem],
        scratch_shapes=[
            pltpu.VMEM((8 * packed_rows + 8, 128), jnp.float32),
            pltpu.VMEM((256, 128), jnp.float32),
            pltpu.VMEM((8, 256), jnp.float32),
            pltpu.VMEM((8, 256), jnp.float32),
            pltpu.VMEM((128, 128), jnp.float32),
            pltpu.VMEM((8, 256), jnp.float32),
            pltpu.VMEM((2, 128, 256), jnp.float32),
            pltpu.VMEM((2, 256, 256), jnp.bfloat16),
            pltpu.VMEM((2, 2, 32, 128), jnp.bfloat16),
            pltpu.SMEM(slots.shape, jnp.int32),
            pltpu.SemaphoreType.DMA,
        ],
        compiler_params=pltpu.CompilerParams(vmem_limit_bytes=52 * MIB),
        name="render",
    )(counts, slots, packed, pixel_basis())


def surface_kernel(maps, out, halo, send_sem, recv_sem):
    row = lax.axis_index("rows")
    col = lax.axis_index("cols")
    sides = [
        (row > 0, (row - 1, col), row < 15),
        (row < 15, (row + 1, col), row > 0),
        (col > 0, (row, col - 1), col < 7),
        (col < 7, (row, col + 1), col > 0),
    ]
    barrier = pltpu.get_barrier_semaphore()
    for there, device, _ in sides:

        @pl.when(there)
        def _(device=device):
            pl.semaphore_signal(
                barrier, inc=1, device_id=device, device_id_type=pl.DeviceIdType.MESH
            )

    neighbours = sum(there.astype(jnp.int32) for there, _, _ in sides)
    pl.semaphore_wait(barrier, neighbours)

    def copy(n, device):
        part = (slice(None), pl.ds(0, 8)) if n == 0 else (slice(None), pl.ds(56, 8))
        source, target = maps.at[:, 0], halo.at[n]
        if n < 2:
            source, target = source.at[part], target.at[part]
        return pltpu.make_async_remote_copy(
            src_ref=source,
            dst_ref=target,
            send_sem=send_sem.at[n],
            recv_sem=recv_sem.at[n],
            device_id=device,
            device_id_type=pl.DeviceIdType.MESH,
        )

    for n, (there, device, _) in enumerate(sides):

        @pl.when(there)
        def _(n=n, device=device):
            copy(n, device).start()

    for n, (there, device, source) in enumerate(sides):

        @pl.when(source)
        def _(n=n):
            copy(n, sides[n ^ 1][1]).wait_recv()

    y = lax.broadcasted_iota(jnp.int32, (64, 128), 0)
    x = lax.broadcasted_iota(jnp.int32, (64, 128), 1)
    for view in range(2):
        depth = maps[view, 0]
        below = jnp.where(row < 15, halo[0, view, 0:1, :], 0.0)
        above = jnp.where(row > 0, halo[1, view, 63:64, :], 0.0)
        right = jnp.where(col < 7, halo[2, view], 0.0)
        left = jnp.where(col > 0, halo[3, view], 0.0)
        north = jnp.where(y == 0, above, pltpu.roll(depth, 1, 0))
        south = jnp.where(y == 63, below, pltpu.roll(depth, 63, 0))
        west = pltpu.roll(jnp.where(x == 127, left, depth), 1, 1)
        east = pltpu.roll(jnp.where(x == 0, right, depth), 127, 1)
        grad_x = 0.5 * (east - west)
        grad_y = 0.5 * (south - north)
        inverse = 1.0 / jnp.sqrt(grad_x * grad_x + grad_y * grad_y + 1.0)
        slope = maps[view, 3] - maps[view, 1] * grad_x - maps[view, 2] * grad_y
        out[view] = 1.0 - slope * inverse

    for n, (there, device, _) in enumerate(sides):

        @pl.when(there)
        def _(n=n, device=device):
            copy(n, device).wait_send()


def consistency_map(maps):
    vmem = pl.BlockSpec(memory_space=pltpu.VMEM)
    return pl.pallas_call(
        surface_kernel,
        out_shape=jax.ShapeDtypeStruct((2, 64, 128), jnp.float32),
        in_specs=[vmem],
        out_specs=vmem,
        scratch_shapes=[
            pltpu.VMEM((4, 2, 64, 128), jnp.float32),
            pltpu.SemaphoreType.DMA((4,)),
            pltpu.SemaphoreType.DMA((4,)),
        ],
        compiler_params=pltpu.CompilerParams(collective_id=0, has_side_effects=True),
        name="surface",
    )(maps)


def shade(position, sh_coeffs, camera):
    offset = position[None, :, :] - camera[:, :, None]
    distance = jnp.sqrt(jnp.sum(offset * offset, axis=1, keepdims=True))
    direction = offset / distance
    dir_x = direction[:, 0]
    dir_y = direction[:, 1]
    dir_z = direction[:, 2]
    sq_x = dir_x * dir_x
    sq_y = dir_y * dir_y
    sq_z = dir_z * dir_z
    sh_basis = jnp.stack(
        [
            jnp.full_like(dir_x, sh_first),
            -sh_second * dir_y,
            sh_second * dir_z,
            -sh_second * dir_x,
            sh_third[0] * dir_x * dir_y,
            sh_third[1] * dir_y * dir_z,
            sh_third[2] * (2.0 * sq_z - sq_x - sq_y),
            sh_third[3] * dir_x * dir_z,
            sh_third[4] * (sq_x - sq_y),
            sh_fourth[0] * dir_y * (3.0 * sq_x - sq_y),
            sh_fourth[1] * dir_x * dir_y * dir_z,
            sh_fourth[2] * dir_y * (4.0 * sq_z - sq_x - sq_y),
            sh_fourth[3] * dir_z * (2.0 * sq_z - 3.0 * sq_x - 3.0 * sq_y),
            sh_fourth[4] * dir_x * (4.0 * sq_z - sq_x - sq_y),
            sh_fourth[5] * dir_z * (sq_x - sq_y),
            sh_fourth[6] * dir_x * (sq_x - 3.0 * sq_y),
        ],
        axis=1,
    )
    coefficients = sh_coeffs.reshape(3, 16, -1)
    colour = 0.5 + jnp.sum(sh_basis[:, None] * coefficients[None], axis=2)
    return jnp.maximum(colour, 0.0).reshape(-1, position.shape[1])


def composite(table_rows, slot_lists, lengths, view_index, view_count, block_count, block_size):
    tile_rows, tile_cols, slot_count = slot_lists.shape
    tile_count = tile_rows * tile_cols
    slot_index = slot_lists.reshape(tile_count, slot_count)
    live_count = lengths.reshape(tile_count)
    pixel_ids = jnp.arange(256, dtype=jnp.int32)
    local_x = ((pixel_ids % 16).astype(jnp.float32) - 7.5) / 8.0
    local_y = ((pixel_ids // 16).astype(jnp.float32) - 7.5) / 8.0
    positions = jnp.arange(block_size, dtype=jnp.int32)
    earlier = (positions[:, None] < positions[None, :]).astype(jnp.float32)
    feature_rows = (
        [10 * view_count + 1 + 3 * view_index + k for k in range(3)]
        + [6 * view_count + 1 + view_index]
        + [7 * view_count + 1 + 3 * view_index + k for k in range(3)]
    )

    def block_step(block_index, state):
        totals, log_before = state
        first_slot = block_index * block_size
        picked_index = lax.dynamic_slice_in_dim(slot_index, first_slot, block_size, 1)
        picked = jnp.take(table_rows, picked_index.reshape(-1), axis=0)
        picked = picked.reshape(tile_count, block_size, table_rows.shape[1]).transpose(2, 0, 1)
        part_map = picked[6 * view_index : 6 * view_index + 6]
        part_opacity = picked[6 * view_count]
        part_features = jnp.stack([picked[row] for row in feature_rows], 0)
        live_mask = ((first_slot + positions)[None, :] < live_count[:, None]).astype(jnp.float32)
        coord_u = (
            part_map[0][:, None, :] * local_x[None, :, None]
            + part_map[1][:, None, :] * local_y[None, :, None]
            + part_map[2][:, None, :]
        )
        coord_w = (
            part_map[3][:, None, :] * local_x[None, :, None]
            + part_map[4][:, None, :] * local_y[None, :, None]
            + part_map[5][:, None, :]
        )
        alphas = part_opacity[:, None, :] * jnp.exp(-0.5 * (coord_u * coord_u + coord_w * coord_w))
        log_keep = jnp.log1p(-alphas) * live_mask[:, None, :]
        before = log_before[:, :, None] + jnp.einsum(
            "tps,sq->tpq", log_keep, earlier, precision=lax.Precision.HIGHEST
        )
        weight = alphas * jnp.exp(before) * live_mask[:, None, :]
        totals = totals + jnp.einsum(
            "fts,tps->tfp", part_features, weight, precision=lax.Precision.HIGHEST
        )
        return (totals, log_before + jnp.sum(log_keep, axis=2))

    start_state = (
        jnp.zeros((tile_count, 7, 256), jnp.float32),
        jnp.zeros((tile_count, 256), jnp.float32),
    )
    totals, unused_log = lax.fori_loop(0, block_count, block_step, start_state)
    return (
        totals.reshape(tile_rows, tile_cols, 7, 16, 16)
        .transpose(2, 0, 3, 1, 4)
        .reshape(7, tile_rows * 16, tile_cols * 16)
    )


def general(
    splat_map,
    opacity,
    depths,
    normals,
    position,
    sh_coeffs,
    camera,
    requests,
    tile_lists,
    list_lengths,
):
    view_count = camera.shape[0]
    device_count = requests.shape[1]
    capacity = requests.shape[2]
    asked_for = lax.all_to_all(requests, ("rows", "cols"), split_axis=1, concat_axis=0, tiled=True)
    wanted = asked_for.reshape(-1)
    geometry_count = 10 * view_count + 1
    source_table = jnp.concatenate(
        [splat_map, opacity[None, :], depths, normals, position, sh_coeffs], 0
    ).T
    gathered = jnp.take(source_table, wanted, axis=0).T
    outgoing = jnp.concatenate(
        [
            gathered[:geometry_count],
            shade(
                gathered[geometry_count : geometry_count + 3],
                gathered[geometry_count + 3 :],
                camera,
            ),
        ],
        0,
    )
    field_rows = outgoing.shape[0]
    arrived = lax.all_to_all(
        outgoing.reshape(field_rows, device_count, capacity),
        ("rows", "cols"),
        split_axis=1,
        concat_axis=1,
        tiled=True,
    ).reshape(field_rows, device_count * capacity)
    padded_count = (field_rows + 7) // 8 * 8
    table_rows = jnp.pad(arrived, ((0, padded_count - field_rows), (0, 0))).T
    slot_count = tile_lists.shape[-1]
    block_size = min(128, slot_count)
    feature_maps = jnp.stack(
        [
            composite(
                table_rows,
                tile_lists[view_index],
                list_lengths[view_index],
                view_index,
                view_count,
                slot_count // block_size,
                block_size,
            )
            for view_index in range(view_count)
        ]
    )
    return feature_maps[:, :3], feature_maps[:, 3:]


def shards(
    splat_map,
    opacity,
    depths,
    normals,
    position,
    sh_coeffs,
    camera,
    requests,
    tile_lists,
    list_lengths,
):
    lengths = list_lengths.reshape(-1)
    lists = tile_lists.reshape(256, 128)
    message, ranks = plan(lengths, lists, requests[0])
    asked_for = lax.all_to_all(message, ("rows", "cols"), split_axis=0, concat_axis=0, tiled=True)
    slots = place(lengths, lists, ranks)
    outgoing = serve(
        asked_for.reshape(-1), splat_map, opacity, depths, normals, position, sh_coeffs, camera
    )
    arrived = lax.all_to_all(
        outgoing.reshape(128, ROWS, 128), ("rows", "cols"), split_axis=0, concat_axis=0, tiled=True
    ).reshape(128 * ROWS, 128)

    def fast():
        return render((lengths + 127) // 128, slots.reshape(-1), arrived)

    def slow():
        return general(
            splat_map,
            opacity,
            depths,
            normals,
            position,
            sh_coeffs,
            camera,
            requests,
            tile_lists,
            list_lengths,
        )

    image, maps = lax.cond(jnp.max(asked_for[:, 255]) > 0, slow, fast)
    return (image, consistency_map(maps))


def solution(mesh):
    in_specs = (
        P(None, ("rows", "cols")),
        P(("rows", "cols")),
        P(None, ("rows", "cols")),
        P(None, ("rows", "cols")),
        P(None, ("rows", "cols")),
        P(None, ("rows", "cols")),
        P(),
        P(("rows", "cols"), None, None),
        P(None, "rows", "cols", None),
        P(None, "rows", "cols"),
    )
    out_specs = (P(None, None, "rows", "cols"), P(None, "rows", "cols"))
    return jax.shard_map(shards, mesh=mesh, in_specs=in_specs, out_specs=out_specs, check_vma=False)
```
